128 devices in a mesh: row: 8 (over y, core), col: 16 (over x, z).
Axes of the slice: x: 4, y: 4, z: 4, core: 2. Of those that a mesh axis runs over, the one named last changes fastest.
Arguments:
- factor: float32 [24, 1048576], P(None, ('row', 'col')), may hold values from -1.2 to 1.2
- prior: float32 [24, 1048576], P(None, ('row', 'col')), may hold values from -1.2 to 1.2
- tile_src: int32 [128, 384], P(('row', 'col')), may hold values from 0 to 63
- tile_dst: int32 [128, 384], P(('row', 'col')), may hold values from 0 to 63
- tile_count: int32 [128], P(('row', 'col')), may hold values from 96 to 384, as said below
- tile_vals: bfloat16 [49152, 128, 128], P(('row', 'col'))
- sep_idx: int32 [128, 4, 256], P(('row', 'col')), may hold values from 0 to 8191, as said below
- sep_count: int32 [128, 4], P(('row', 'col')), may hold values from 64 to 256, as said below
- couple: bfloat16 [128, 4, 256, 256], P(('row', 'col')), may hold values from -0.1875 to 0.1875
- masks: int32 [4], replicated, may hold values from 1 to 127, as said below
Outputs:
- new_factor: float32 [24, 1048576], P(None, ('row', 'col'))
- momentum: float32 [], replicated
- energy: float32 [], replicated
The draws below stay inside these ranges and needn't reach their ends.
Inputs may be any that keep to these rules, and one draw needn't show every extreme that they name: `tile_count`: some partition has all 384 slots live; slots at or beyond a partition's count are padding. `sep_idx`: distinct within one partition and round. `sep_count`: in every round some partition has all 256 slots live. masks[0] is 127, masks[1] is 64 and the last round's mask is 1.
All inputs are finite; a program needn't handle non-finite values.
Results may differ from the reference program's by a relative error of at most 0.0031.
Values may be sent and summed in bfloat16 or wider, within the bound.
No kernel may reach another device: no remote copies, remote signals or barrier semaphores. Data moves between devices by JAX's collectives and lax.ppermute only.
A program may use at most 128 MiB of HBM per device.

```python
import jax
import jax.numpy as jnp
from jax import lax

R = 24
TILE = 128
ROUNDS = 4
ITERS = 2
NODE_DEV = 8192
TILES_DEV = 384
SEP = 256
PARTS_SIZE = 128
NB = 64
NODES = 1048576


def draw_tile_vals(key, part):
    position = jnp.arange(PARTS_SIZE, dtype=jnp.float32) / max(PARTS_SIZE - 1, 1)
    spread = 0.6 * (1.0 + 2.0 * position) / jnp.sqrt(5.0 * TILE)
    scaling = jnp.repeat(spread, TILES_DEV)[:, None, None]
    base = jax.random.normal(key, (PARTS_SIZE * TILES_DEV, TILE, TILE), jnp.float32)
    return (base * scaling).astype(jnp.bfloat16)


def draw_sep_idx(key, part):
    subkeys = jax.random.split(jax.random.fold_in(key, 11), PARTS_SIZE * ROUNDS)

    def pick_nodes(subkey):
        return jax.random.permutation(subkey, NODE_DEV)[:SEP]
    chosen = jax.vmap(pick_nodes)(subkeys)
    return chosen.reshape(PARTS_SIZE, ROUNDS, SEP).astype(jnp.int32)


def draw_sep_count(key, part):
    first_key = jax.random.fold_in(key, 21)
    second_key = jax.random.fold_in(key, 22)
    base = jax.random.randint(first_key, (PARTS_SIZE, ROUNDS), SEP // 4, SEP + 1)
    fullest = jax.random.randint(second_key, (ROUNDS,), 0, PARTS_SIZE)
    hit = jnp.arange(PARTS_SIZE, dtype=jnp.int32)[:, None] == fullest[None, :]
    return jnp.where(hit, SEP, base).astype(jnp.int32)


def draw_tile_count(key, part):
    first_key = jax.random.fold_in(key, 31)
    second_key = jax.random.fold_in(key, 32)
    shifts = jax.random.randint(first_key, (PARTS_SIZE,), 0, 3)
    base = jnp.right_shift(jnp.full((PARTS_SIZE,), TILES_DEV, jnp.int32), shifts)
    fullest = jax.random.randint(second_key, (), 0, PARTS_SIZE)
    return jnp.where(jnp.arange(PARTS_SIZE, dtype=jnp.int32) == fullest, TILES_DEV, base).astype(jnp.int32)


def draw_masks(key, part):
    middle = jax.random.randint(jax.random.fold_in(key, 41), (ROUNDS,), 1, PARTS_SIZE)
    middle = middle.at[0].set(PARTS_SIZE - 1)
    middle = middle.at[1].set(PARTS_SIZE // 2)
    middle = middle.at[ROUNDS - 1].set(1)
    return middle.astype(jnp.int32)


def place_ends(drawn, stream_key, low, largest):
    longest = drawn.shape.index(max(drawn.shape))
    spots = []
    for shift in (0, 1):
        where = [jax.random.randint(jax.random.fold_in(stream_key, axis), (), 0, length) for axis, length in enumerate(drawn.shape)]
        where[longest] = (where[longest] + shift) % drawn.shape[longest]
        spots.append(tuple(where))
    return drawn.at[spots[0]].set(low).at[spots[1]].set(largest)


def steps_of(stream_key, dims, shards, smallest, top_value):
    def one(dim, shards_of):
        heights = jax.random.uniform(jax.random.fold_in(jax.random.fold_in(stream_key, 6), dim), (shards_of,), jnp.float32, smallest / len(shards), top_value / len(shards))
        return jnp.repeat(jnp.exp(heights), dims[dim] // shards_of).reshape((-1,) + (1,) * (len(dims) - dim - 1))

    loudness = one(*shards[0])
    for cut in shards[1:]:
        loudness = loudness * one(*cut)
    return loudness


def scatter_about(own_key, dims, width, bound, cuts=(), kind=jnp.bfloat16):
    values = width * jax.random.normal(own_key, dims, jnp.float32)
    if cuts:
        values = values * steps_of(own_key, dims, cuts, -0.22, 0.18)
    return jnp.clip(values, -bound, bound).astype(kind)


def setup_inputs(seed: int = 0) -> dict:
    arg_keys = jax.random.split(jax.random.key(seed), 11)
    factor = scatter_about(arg_keys[0], (R, NODES), 0.2, 1.2, ((1, 128),), jnp.float32)
    prior = scatter_about(arg_keys[1], (R, NODES), 0.2, 1.2, ((1, 128),), jnp.float32)
    tile_src = place_ends(jax.random.randint(arg_keys[2], (PARTS_SIZE, TILES_DEV), 0, NB), jax.random.fold_in(arg_keys[2], 1), 0, NB - 1).astype(jnp.int32)
    tile_dst = place_ends(jax.random.randint(arg_keys[3], (PARTS_SIZE, TILES_DEV), 0, NB), jax.random.fold_in(arg_keys[3], 1), 0, NB - 1).astype(jnp.int32)
    tile_count = draw_tile_count(jax.random.fold_in(arg_keys[10], 71), 0)
    tile_vals = draw_tile_vals(jax.random.fold_in(arg_keys[10], 71), 0)
    sep_idx = draw_sep_idx(jax.random.fold_in(arg_keys[10], 71), 0)
    sep_count = draw_sep_count(jax.random.fold_in(arg_keys[10], 71), 0)
    couple = scatter_about(arg_keys[8], (PARTS_SIZE, ROUNDS, SEP, SEP), (4 * SEP) ** -0.5, 0.1875, ((0, 128),))
    masks = draw_masks(jax.random.fold_in(arg_keys[10], 71), 0)
    return {"factor": factor, "prior": prior, "tile_src": tile_src, "tile_dst": tile_dst, "tile_count": tile_count, "tile_vals": tile_vals, "sep_idx": sep_idx, "sep_count": sep_count, "couple": couple, "masks": masks}


MOMENTUM_CAP = 0.9

def tile_apply(inputs):
    grouped, sources, targets, live_count, values = inputs
    picked = jnp.take(grouped, sources, axis=1).astype(jnp.float32)
    products = jnp.einsum('rtk,tkc->rtc', picked, values.astype(jnp.float32), precision=lax.Precision.HIGHEST)
    live_tiles = (jnp.arange(sources.shape[0]) < live_count).astype(jnp.float32)
    dst_table = (targets[None, :] == jnp.arange(grouped.shape[1], dtype=jnp.int32)[:, None]).astype(jnp.float32) * live_tiles[None, :]
    return jnp.einsum('bt,rtc->rbc', dst_table, products, precision=lax.Precision.HIGHEST)

def add_columns(target, columns, extra):
    return target.at[:, columns].add(extra)

def operate(packed, tile_src, tile_dst, tile_count, tile_vals, sep_idx, sep_count, couple, masks):
    grouped_all = packed.reshape(R, PARTS_SIZE, NB, TILE).transpose(1, 0, 2, 3)
    values_all = tile_vals.reshape(PARTS_SIZE, TILES_DEV, TILE, TILE)
    applied_dev = lax.map(tile_apply, (grouped_all, tile_src, tile_dst, tile_count, values_all))
    applied_dev = applied_dev.reshape(PARTS_SIZE, R, NODE_DEV)
    packed_dev = packed.reshape(R, PARTS_SIZE, NODE_DEV).transpose(1, 0, 2)
    for rnd in range(ROUNDS):
        columns = sep_idx[:, rnd, :]
        keep = jnp.arange(SEP, dtype=jnp.int32)[None, :] < sep_count[:, rnd][:, None]
        picked = jnp.take_along_axis(packed_dev, columns[:, None, :], axis=2)
        sent = jnp.where(keep[:, None, :], picked, jnp.zeros_like(picked))
        partner = jnp.arange(PARTS_SIZE, dtype=jnp.int32) ^ masks[rnd]
        received = sent[partner].astype(jnp.float32)
        extra = jnp.einsum('prs,pst->prt', received, couple[:, rnd].astype(jnp.float32), precision=lax.Precision.HIGHEST)
        extra = jnp.where(keep[:, None, :], extra, jnp.zeros_like(extra))
        applied_dev = jax.vmap(add_columns)(applied_dev, columns, extra)
    return applied_dev.transpose(1, 0, 2).reshape(R, NODES)

def reference(factor, prior, tile_src, tile_dst, tile_count, tile_vals, sep_idx, sep_count, couple, masks):
    current = factor
    previous = prior
    beta = jnp.float32(0.5 * MOMENTUM_CAP)
    energy = jnp.float32(0.0)
    for iterate in range(ITERS):
        blend = current + beta * (current - previous)
        packed = blend.astype(jnp.bfloat16)
        applied = operate(packed, tile_src, tile_dst, tile_count, tile_vals, sep_idx, sep_count, couple, masks)
        moved = blend + applied
        length = jnp.sqrt(lax.optimization_barrier(jnp.sum(moved * moved, axis=0, keepdims=True)))
        updated = moved / jnp.maximum(length, 1.0)
        change = jnp.sum(applied * (updated - current))
        energy = jnp.sum(applied * updated) / NODES
        beta = MOMENTUM_CAP * 0.5 * (1.0 + jnp.tanh(change / NODES))
        previous = current
        current = updated
    return (current, beta, energy)
```

```python
import jax
import jax.numpy as jnp
from jax import lax
from jax.experimental import pallas as pl
from jax.experimental.pallas import tpu as pltpu
from jax.sharding import PartitionSpec as P

TILE = 128
MOMENTUM_CAP = 0.9
BETA0 = 0.5 * MOMENTUM_CAP
AXES = ("row", "col")
VMEM_LIMIT = 48 * 1024 * 1024
SMEM = pl.BlockSpec(memory_space=pltpu.SMEM)
VMEM = pl.BlockSpec(memory_space=pltpu.VMEM)


def block_of(b):
    return pl.ds(pl.multiple_of(b * TILE, TILE), TILE)


def gather_columns(work, idx_ref, count_ref, outs):
    blocks, comps, _ = work.shape
    lane = lax.broadcasted_iota(jnp.int32, (1, TILE), 1)
    for k, out in enumerate(outs):
        slots = out.shape[1]
        if out.shape[0] > comps:
            out[...] = jnp.zeros_like(out)
        for h in range(slots // TILE):
            idx = idx_ref[k : k + 1, h * TILE : (h + 1) * TILE]
            live = lane + h * TILE < count_ref[0, k]
            home = jnp.broadcast_to(jnp.where(live, idx // TILE, -1), (comps, TILE))
            spot = jnp.broadcast_to(idx % TILE, (comps, TILE))

            def step(b, found, home=home, spot=spot):
                moved = jnp.take_along_axis(work[b], spot, axis=1, mode="promise_in_bounds")
                return jnp.where(home == b, moved, found)

            found = lax.fori_loop(0, blocks, step, jnp.zeros((comps, TILE), jnp.float32), unroll=8)
            rows = out.shape[0]
            if rows > comps:
                found = jnp.concatenate([found, jnp.zeros((rows - comps, TILE), jnp.float32)], axis=0)
            out[:, h * TILE : (h + 1) * TILE] = found.astype(out.dtype)


def prepare_kernel(factor, prior, idx_ref, count_ref, packed, *rest):
    outs, work = rest[:-1], rest[-1]
    blocks = packed.shape[0]
    comps = factor.shape[0]
    pad = jnp.zeros((packed.shape[1] - comps, TILE), jnp.float32)

    def step(b, _):
        f = factor[:, block_of(b)]
        blend = f + BETA0 * (f - prior[:, block_of(b)])
        work[b] = blend
        packed[b] = jnp.concatenate([blend, pad], axis=0).astype(packed.dtype)
        return 0

    lax.fori_loop(0, blocks, step, 0, unroll=4)
    gather_columns(work, idx_ref, count_ref, outs)


def prepare(factor, prior, sep_idx, sep_count):
    comps, nodes = factor.shape
    rounds, slots = sep_idx.shape
    rows = 32
    outs = pl.pallas_call(
        prepare_kernel,
        out_shape=[jax.ShapeDtypeStruct((nodes // TILE, rows, TILE), jnp.bfloat16)]
        + [jax.ShapeDtypeStruct((rows, slots), jnp.bfloat16)] * rounds,
        in_specs=[VMEM, VMEM, VMEM, SMEM],
        out_specs=[VMEM] * (1 + rounds),
        scratch_shapes=[pltpu.VMEM((nodes // TILE, comps, TILE), jnp.float32)],
        compiler_params=pltpu.CompilerParams(vmem_limit_bytes=VMEM_LIMIT),
        name="prepare",
    )(factor, prior, sep_idx, sep_count)
    return outs[0], list(outs[1:])


def tile_kernel(keep, group, src, dst, count, packed, vals, total):
    step = pl.program_id(0)
    chunk = vals.shape[0]
    spare = packed.shape[0]

    @pl.when(step == 0)
    def _():
        total[...] = jnp.zeros_like(total)

    def one(g, _):
        base = g * group
        first = step * chunk + base
        products = [
            jnp.dot(packed[src[0, first + j]], vals[base + j], preferred_element_type=jnp.float32)
            for j in range(group)
        ]
        for j in range(group):
            to = jnp.where(first + j < count[0], dst[0, first + j], spare)
            total[to] += products[j][:keep]
        return 0

    lax.fori_loop(0, chunk // group, one, 0)


def tile_product(packed, tile_src, tile_dst, tile_count, tile_vals, keep):
    blocks, rows, _ = packed.shape
    slots = tile_vals.shape[0]
    chunk, group = 32, 16

    def body(*refs):
        tile_kernel(keep, group, *refs)

    return pl.pallas_call(
        body,
        out_shape=jax.ShapeDtypeStruct((blocks + 1, keep, TILE), jnp.float32),
        grid_spec=pltpu.PrefetchScalarGridSpec(
            num_scalar_prefetch=3,
            grid=(slots // chunk,),
            in_specs=[
                pl.BlockSpec((blocks, rows, TILE), lambda i, *_: (0, 0, 0)),
                pl.BlockSpec((chunk, TILE, TILE), lambda i, *_: (i, 0, 0)),
            ],
            out_specs=pl.BlockSpec((blocks + 1, keep, TILE), lambda i, *_: (0, 0, 0)),
        ),
        compiler_params=pltpu.CompilerParams(vmem_limit_bytes=VMEM_LIMIT),
        cost_estimate=pl.CostEstimate(
            flops=2 * slots * rows * TILE * TILE,
            bytes_accessed=slots * TILE * TILE * 2 + blocks * rows * TILE * 8,
            transcendentals=0,
        ),
        name="tile_product",
    )(tile_src, tile_dst, tile_count, packed, tile_vals)


def scatter_rows(extra_rows, idx_smem, spread):
    rounds, slots = idx_smem.shape
    spread[...] = jnp.zeros_like(spread)
    for k in range(rounds):

        def step(c, _, k=k):
            at = [idx_smem[k, c * 8 + j] for j in range(8)]
            new = [
                spread[pl.ds(at[j], 1), :] + extra_rows[pl.ds(k * slots + c * 8 + j, 1), :]
                for j in range(8)
            ]
            for j in range(8):
                spread[pl.ds(at[j], 1), :] = new[j]
            return 0

        lax.fori_loop(0, slots // 8, step, 0, unroll=2)


def couple_rows(received, couple, count_ref, extra_rows, combine):
    for k, ref in enumerate(received):
        slots = ref.shape[1]
        extra = combine(jnp.dot(ref[...], couple[k], preferred_element_type=jnp.float32))
        slot = lax.broadcasted_iota(jnp.int32, extra.shape, 1)
        extra = jnp.where(slot < count_ref[0, k], extra, 0.0)
        fill = jnp.zeros((TILE - extra.shape[0], slots), jnp.float32)
        extra_rows[k * slots : (k + 1) * slots, :] = jnp.concatenate([extra, fill], axis=0).T


def fold(change, total):
    a = jnp.sum(change, axis=0, keepdims=True)
    b = jnp.sum(total, axis=0, keepdims=True)
    a = a + pltpu.roll(a, 64, 1)
    b = b + pltpu.roll(b, 64, 1)
    lane = lax.broadcasted_iota(jnp.int32, a.shape, 1)
    return jnp.where(lane < 64, a, b)


def first_kernel(factor, prior, total, r0, r1, r2, r3, couple, idx_ref, idx_smem, count_ref,
                 updated, packed, part, s0, s1, s2, s3, spread, extra_rows, work):
    comps = factor.shape[0]
    blocks = packed.shape[0]
    couple_rows((r0, r1, r2, r3), couple, count_ref, extra_rows, lambda e: e[:comps])
    scatter_rows(extra_rows, idx_smem, spread)

    def step(b, sums):
        f = factor[:, block_of(b)]
        blend = f + BETA0 * (f - prior[:, block_of(b)])
        applied = total[b] + spread[block_of(b), :].T[:comps]
        moved = blend + applied
        square = jnp.sum(moved * moved, axis=0, keepdims=True)
        u = moved * lax.rsqrt(jnp.maximum(square, 1.0))
        d = u - f
        updated[:, block_of(b)] = u
        both = jnp.concatenate([u + BETA0 * d, d], axis=0)
        work[b] = both
        packed[b] = both.astype(packed.dtype)
        return sums + applied * d

    sums = lax.fori_loop(0, blocks, step, jnp.zeros((comps, TILE), jnp.float32), unroll=2)
    part[...] = jnp.broadcast_to(fold(sums, sums), part.shape)
    gather_columns(work, idx_ref, count_ref, (s0, s1, s2, s3))


def finish_first(factor, prior, total, received, couple, sep_idx, sep_count, parts):
    comps, nodes = factor.shape
    rounds, slots = sep_idx.shape
    f32 = jnp.float32
    outs = pl.pallas_call(
        first_kernel,
        out_shape=[
            jax.ShapeDtypeStruct((comps, nodes), f32),
            jax.ShapeDtypeStruct((nodes // TILE, 2 * comps, TILE), jnp.bfloat16),
            jax.ShapeDtypeStruct((parts, TILE), f32),
        ]
        + [jax.ShapeDtypeStruct((2 * comps, slots), jnp.bfloat16)] * rounds,
        in_specs=[VMEM] * 9 + [SMEM, SMEM],
        out_specs=[VMEM] * (3 + rounds),
        scratch_shapes=[
            pltpu.VMEM((nodes, TILE), f32),
            pltpu.VMEM((rounds * slots, TILE), f32),
            pltpu.VMEM((nodes // TILE, 2 * comps, TILE), f32),
        ],
        compiler_params=pltpu.CompilerParams(vmem_limit_bytes=VMEM_LIMIT),
        name="finish_first",
    )(factor, prior, total, *received, couple, sep_idx, sep_idx, sep_count)
    return outs[0], outs[1], outs[2], list(outs[3:])


def beta_of(change, nodes_all):
    return MOMENTUM_CAP * 0.5 * (1.0 + jnp.tanh(change / nodes_all))


def last_kernel(nodes_all, current, factor, parts, total, r0, r1, r2, r3, couple, idx_smem, count_ref,
                updated, part, spread, extra_rows):
    comps = current.shape[0]
    blocks = total.shape[0] - 1
    lane = lax.broadcasted_iota(jnp.int32, (1, TILE), 1)
    summed = jnp.sum(parts[...], axis=0, keepdims=True)
    change = jnp.sum(jnp.where(lane < 64, summed, 0.0), axis=1, keepdims=True)
    beta = beta_of(change, nodes_all)
    gap = beta - BETA0
    couple_rows((r0, r1, r2, r3), couple, count_ref, extra_rows, lambda e: e[:comps] + gap * e[comps:])
    scatter_rows(extra_rows, idx_smem, spread)

    def step(b, sums):
        u = current[:, block_of(b)]
        blend = u + beta * (u - factor[:, block_of(b)])
        both = total[b]
        applied = both[:comps] + gap * both[comps:] + spread[block_of(b), :].T[:comps]
        moved = blend + applied
        square = jnp.sum(moved * moved, axis=0, keepdims=True)
        new = moved * lax.rsqrt(jnp.maximum(square, 1.0))
        updated[:, block_of(b)] = new
        return sums[0] + applied * (new - u), sums[1] + applied * new

    zero = jnp.zeros((comps, TILE), jnp.float32)
    sums = lax.fori_loop(0, blocks, step, (zero, zero), unroll=2)
    part[...] = jnp.broadcast_to(fold(*sums), part.shape)


def finish_last(current, factor, parts, total, received, couple, sep_idx, sep_count, nodes_all):
    comps, nodes = factor.shape
    rounds, slots = sep_idx.shape
    f32 = jnp.float32

    def body(*refs):
        last_kernel(nodes_all, *refs)

    return pl.pallas_call(
        body,
        out_shape=[
            jax.ShapeDtypeStruct((comps, nodes), f32),
            jax.ShapeDtypeStruct(parts.shape, f32),
        ],
        in_specs=[VMEM] * 9 + [SMEM, SMEM],
        out_specs=[VMEM] * 2,
        scratch_shapes=[
            pltpu.VMEM((nodes, TILE), f32),
            pltpu.VMEM((rounds * slots, TILE), f32),
        ],
        compiler_params=pltpu.CompilerParams(vmem_limit_bytes=VMEM_LIMIT),
        name="finish_last",
    )(current, factor, parts, total, *received, couple, sep_idx, sep_count)


def hop(value, mask, size):
    return lax.ppermute(value, AXES, [(i, i ^ mask) for i in range(size)])


def exchange(sent, masks, size, low):
    def stay(value):
        return value

    first = hop(sent[0], size - 1, size)
    second = hop(sent[1], size // 2, size)
    fourth = hop(sent[3], 1, size)
    mask = masks[2]
    third = lax.switch(
        mask % low, [stay] + [lambda v, m=m: hop(v, m, size) for m in range(1, low)], sent[2]
    )
    third = lax.switch(
        mask // low,
        [stay] + [lambda v, m=m: hop(v, m * low, size) for m in range(1, size // low)],
        third,
    )
    return [first, second, third, fourth]


def share(part):
    return lax.all_to_all(part, AXES, 0, 0, tiled=True)


def local(
    factor, prior, tile_src, tile_dst, tile_count, tile_vals, sep_idx, sep_count, couple, masks
):
    size = lax.axis_size(AXES)
    low = lax.axis_size("col")
    comps, nodes = factor.shape
    nodes_all = size * nodes
    idx, pairs = sep_idx[0], couple[0]
    packed, sent = prepare(factor, prior, idx, sep_count)
    received = exchange(sent, masks, size, low)
    total = tile_product(packed, tile_src, tile_dst, tile_count, tile_vals, comps)
    current, packed, part, sent = finish_first(
        factor, prior, total, received, pairs, idx, sep_count, size
    )
    parts = share(part)
    received = exchange(sent, masks, size, low)
    total = tile_product(packed, tile_src, tile_dst, tile_count, tile_vals, 2 * comps)
    updated, part = finish_last(
        current, factor, parts, total, received, pairs, idx, sep_count, nodes_all
    )
    summed = jnp.sum(share(part), axis=0)
    beta = beta_of(jnp.sum(summed[:64]), nodes_all)
    energy = jnp.sum(summed[64:]) / nodes_all
    return updated, beta, energy


def solution(mesh):
    in_specs = (
        P(None, ("row", "col")),
        P(None, ("row", "col")),
        P(("row", "col"), None),
        P(("row", "col"), None),
        P(("row", "col")),
        P(("row", "col"), None, None),
        P(("row", "col"), None, None),
        P(("row", "col"), None),
        P(("row", "col"), None, None, None),
        P(),
    )
    out_specs = (P(None, ("row", "col")), P(), P())
    return jax.shard_map(local, mesh=mesh, in_specs=in_specs, out_specs=out_specs, check_vma=False)
```

```python
import jax
import jax.numpy as jnp
from jax import lax
from jax.experimental import pallas as pl
from jax.experimental.pallas import tpu as pltpu
from jax.sharding import PartitionSpec as P

TILE = 128
MOMENTUM_CAP = 0.9
BETA0 = 0.5 * MOMENTUM_CAP
AXES = ("row", "col")
MIB = 1024 * 1024
WIDE = 4
BATCH = 16
SMEM = pl.BlockSpec(memory_space=pltpu.SMEM)
VMEM = pl.BlockSpec(memory_space=pltpu.VMEM)
HBM = pl.BlockSpec(memory_space=pltpu.HBM)
PARTS = 4


def span(c):
    return pl.ds(pl.multiple_of(c * WIDE * TILE, WIDE * TILE), WIDE * TILE)


def identity(n):
    row = lax.broadcasted_iota(jnp.int32, (n, n), 0)
    return jnp.where(row == lax.broadcasted_iota(jnp.int32, (n, n), 1), 1.0, 0.0).astype(jnp.bfloat16)


def turn_into(rows_ref, c, eye, values):
    n = eye.shape[0]
    for i in range(values.shape[1] // n):
        turned = lax.dot_general(
            eye, values[:, i * n : (i + 1) * n], (((1,), (1,)), ((), ())),
            preferred_element_type=jnp.float32,
        )
        start = pl.multiple_of(c * WIDE * TILE + i * n, n)
        rows_ref[pl.ds(start, n), : values.shape[0]] = turned


def copy_rows(node_rows, idx_smem, slot_rows):
    rounds, slots = idx_smem.shape
    for k in range(rounds):

        def step(c, _, k=k):
            at = [idx_smem[k, c * BATCH + j] for j in range(BATCH)]
            rows = [node_rows[pl.ds(at[j], 1), :] for j in range(BATCH)]
            for j in range(BATCH):
                slot_rows[pl.ds(k * slots + c * BATCH + j, 1), :] = rows[j]
            return 0

        lax.fori_loop(0, slots // BATCH, step, 0, unroll=2)


def columns(slot_rows, k, count_ref, rows, comps, slots):
    got = slot_rows[k * slots : (k + 1) * slots, :].T[:rows]
    keep = lax.broadcasted_iota(jnp.int32, got.shape, 1) < count_ref[0, k]
    if rows > comps:
        keep = keep & (lax.broadcasted_iota(jnp.int32, got.shape, 0) < comps)
    return jnp.where(keep, got, 0.0).astype(jnp.bfloat16)


def emit(slot_rows, count_ref, outs, own, comps):
    rows, slots = own.shape
    shared = columns(slot_rows, 2, count_ref, rows, comps, slots)
    own[...] = shared
    for k, out in zip((0, 1, 3), outs):
        out[:rows] = columns(slot_rows, k, count_ref, rows, comps, slots)
        out[rows:] = shared


def part_copies(source, target, sems):
    width = source.shape[1] // PARTS
    return [
        pltpu.make_async_copy(
            source.at[:, pl.ds(i * width, width)], target.at[:, pl.ds(i * width, width)], sems.at[i]
        )
        for i in range(PARTS)
    ]


def block_copies(source, target, sems):
    blocks = target.shape[0] // PARTS
    return [
        pltpu.make_async_copy(
            source.at[pl.ds(i * blocks, blocks)], target.at[pl.ds(i * blocks, blocks)], sems.at[i]
        )
        for i in range(PARTS)
    ]


def prepare_kernel(size, masks, factor_hbm, prior_hbm, idx_smem, count_ref,
                   packed, s0, s1, s3, own, branch, source, node_rows, slot_rows, factor, prior, sems):
    f_copies = part_copies(factor_hbm, factor, sems.at[0])
    p_copies = part_copies(prior_hbm, prior, sems.at[1])
    for i in range(PARTS):
        f_copies[i].start()
        p_copies[i].start()
    comps, nodes = factor.shape
    rows = packed.shape[1]
    mask = masks[2]
    top, bottom = (mask >= size // 2).astype(jnp.int32), mask & 1
    source[0] = 2 * top + bottom
    rest = jnp.where(top + bottom == 2, mask ^ (size - 1), mask)
    branch[0] = lax.shift_right_logical(rest & (size // 2 - 1), 1)
    pad = jnp.zeros((rows - comps, WIDE * TILE), jnp.float32)
    eye = identity(2 * TILE)

    def step(c, _):
        f = factor[:, span(c)]
        blend = f + BETA0 * (f - prior[:, span(c)])
        values = jnp.concatenate([blend, pad], axis=0).astype(packed.dtype)
        turn_into(node_rows, c, eye, values)
        for i in range(WIDE):
            packed[c * WIDE + i] = values[:, i * TILE : (i + 1) * TILE]
        return 0

    each = nodes // (WIDE * TILE * PARTS)
    for i in range(PARTS):
        f_copies[i].wait()
        p_copies[i].wait()
        lax.fori_loop(i * each, (i + 1) * each, step, 0, unroll=2)
    copy_rows(node_rows, idx_smem, slot_rows)
    emit(slot_rows, count_ref, (s0, s1, s3), own, comps)


def prepare(masks, factor, prior, sep_idx, sep_count, size):
    comps, nodes = factor.shape
    rounds, slots = sep_idx.shape
    rows = 32

    def body(*refs):
        prepare_kernel(size, *refs)

    both = jax.ShapeDtypeStruct((2 * rows, slots), jnp.bfloat16)
    return pl.pallas_call(
        body,
        out_shape=[
            jax.ShapeDtypeStruct((nodes // TILE, rows, TILE), jnp.bfloat16),
            both,
            both,
            both,
            jax.ShapeDtypeStruct((rows, slots), jnp.bfloat16),
            jax.ShapeDtypeStruct((1,), jnp.int32),
            jax.ShapeDtypeStruct((1,), jnp.int32),
        ],
        in_specs=[SMEM, HBM, HBM, SMEM, SMEM],
        out_specs=[VMEM] * 5 + [SMEM] * 2,
        scratch_shapes=[
            pltpu.VMEM((nodes, TILE), jnp.float32),
            pltpu.VMEM((rounds * slots, TILE), jnp.float32),
            pltpu.VMEM((comps, nodes), jnp.float32),
            pltpu.VMEM((comps, nodes), jnp.float32),
            pltpu.SemaphoreType.DMA((2, PARTS)),
        ],
        compiler_params=pltpu.CompilerParams(vmem_limit_bytes=62 * MIB),
        name="prepare",
    )(masks, factor, prior, sep_idx, sep_count)


def tile_kernel(keep, group, src, dst, count, packed_hbm, vals_hbm, total, packed, vals, sems):
    slots = vals.shape[0]
    groups = slots // group
    spare, rows, _ = packed.shape
    bring = pltpu.make_async_copy(packed_hbm, packed, sems.at[groups])
    bring.start()

    def tiles(g):
        at = pl.ds(g * group, group)
        return pltpu.make_async_copy(vals_hbm.at[at], vals.at[at], sems.at[g])

    for g in range(groups):
        tiles(g).start()
    total[...] = jnp.zeros_like(total)
    bring.wait()

    def one(g, _):
        tiles(g).wait()
        base = g * group
        products = []
        for j in range(0, group, 2):
            left = jnp.concatenate([packed[src[0, base + j]], packed[src[0, base + j + 1]]], axis=0)
            right = jnp.concatenate([vals[base + j], vals[base + j + 1]], axis=1)
            both = jnp.dot(left, right, preferred_element_type=jnp.float32)
            products += [both[:keep, :TILE], both[rows : rows + keep, TILE:]]
        for j in range(group):
            to = jnp.where(base + j < count[0], dst[0, base + j], spare)
            total[to] += products[j]
        return 0

    lax.fori_loop(0, groups, one, 0)


def tile_product(packed, tile_src, tile_dst, tile_count, tile_vals, keep):
    blocks, rows, _ = packed.shape
    slots = tile_vals.shape[0]
    group = 64

    def body(*refs):
        tile_kernel(keep, group, *refs)

    return pl.pallas_call(
        body,
        out_shape=jax.ShapeDtypeStruct((blocks + 1, keep, TILE), jnp.float32),
        in_specs=[SMEM, SMEM, SMEM, HBM, HBM],
        out_specs=VMEM,
        scratch_shapes=[
            pltpu.VMEM(packed.shape, packed.dtype),
            pltpu.VMEM(tile_vals.shape, tile_vals.dtype),
            pltpu.SemaphoreType.DMA((slots // group + 1,)),
        ],
        compiler_params=pltpu.CompilerParams(vmem_limit_bytes=56 * MIB),
        cost_estimate=pl.CostEstimate(
            flops=2 * slots * rows * TILE * TILE,
            bytes_accessed=slots * TILE * TILE * 2 + blocks * rows * TILE * 8,
            transcendentals=0,
        ),
        name="tile_product",
    )(tile_src, tile_dst, tile_count, packed, tile_vals)


def scatter_rows(extra_rows, idx_smem, spread):
    rounds, slots = idx_smem.shape
    spread[...] = jnp.zeros_like(spread)
    for k in range(rounds):

        def step(c, _, k=k):
            at = [idx_smem[k, c * BATCH + j] for j in range(BATCH)]
            new = [
                spread[pl.ds(at[j], 1), :] + extra_rows[pl.ds(k * slots + c * BATCH + j, 1), :]
                for j in range(BATCH)
            ]
            for j in range(BATCH):
                spread[pl.ds(at[j], 1), :] = new[j]
            return 0

        lax.fori_loop(0, slots // BATCH, step, 0, unroll=2)


def couple_rows(rows, received, couple, count_ref, extra_rows, combine):
    for k, ref in enumerate(received):
        slots = ref.shape[1]
        extra = combine(jnp.dot(ref[:rows], couple[k], preferred_element_type=jnp.float32))
        slot = lax.broadcasted_iota(jnp.int32, extra.shape, 1)
        extra = jnp.where(slot < count_ref[0, k], extra, 0.0)
        fill = jnp.zeros((TILE - extra.shape[0], slots), jnp.float32)
        extra_rows[k * slots : (k + 1) * slots, :] = jnp.concatenate([extra, fill], axis=0).T


def wide_total(total, c):
    return jnp.concatenate([total[c * WIDE + i] for i in range(WIDE)], axis=1)


def narrow(sums):
    return sum(sums[:, i * TILE : (i + 1) * TILE] for i in range(WIDE))


def fold(change, total):
    a = jnp.sum(change, axis=0, keepdims=True)
    b = jnp.sum(total, axis=0, keepdims=True)
    a = a + pltpu.roll(a, 64, 1)
    b = b + pltpu.roll(b, 64, 1)
    lane = lax.broadcasted_iota(jnp.int32, a.shape, 1)
    return jnp.where(lane < 64, a, b)


def first_kernel(factor_hbm, prior_hbm, total_hbm, r0, r1, r2, r3, couple_hbm, idx_smem, count_ref,
                 updated_hbm, packed_hbm, part, s0, s1, s3, own, node_rows, slot_rows, updated, packed,
                 factor, prior, total, couple, sems, in_sems):
    bring = pltpu.make_async_copy(couple_hbm, couple, sems.at[PARTS + 1])
    bring.start()
    come = (
        part_copies(factor_hbm, factor, in_sems.at[0]),
        part_copies(prior_hbm, prior, in_sems.at[1]),
        block_copies(total_hbm, total, in_sems.at[2]),
    )
    for i in range(PARTS):
        for copies in come:
            copies[i].start()
    comps, nodes = factor.shape
    bring.wait()
    couple_rows(r2.shape[0], (r0, r1, r2, r3), couple, count_ref, slot_rows, lambda e: e[:comps])
    scatter_rows(slot_rows, idx_smem, node_rows)
    eye = identity(2 * TILE)

    def step(c, sums):
        f = factor[:, span(c)]
        blend = f + BETA0 * (f - prior[:, span(c)])
        applied = wide_total(total, c) + node_rows[span(c), :].T[:comps]
        moved = blend + applied
        square = jnp.sum(moved * moved, axis=0, keepdims=True)
        u = moved * lax.rsqrt(jnp.maximum(square, 1.0))
        d = u - f
        updated[:, span(c)] = u
        both = jnp.concatenate([u + BETA0 * d, d], axis=0).astype(packed.dtype)
        turn_into(node_rows, c, eye, both)
        for i in range(WIDE):
            packed[c * WIDE + i] = both[:, i * TILE : (i + 1) * TILE]
        return sums + applied * d

    copies = part_copies(updated, updated_hbm, sems)
    sums = jnp.zeros((comps, WIDE * TILE), jnp.float32)
    each = nodes // (WIDE * TILE * PARTS)
    for i in range(PARTS):
        for arriving in come:
            arriving[i].wait()
        sums = lax.fori_loop(i * each, (i + 1) * each, step, sums, unroll=2)
        copies[i].start()
    copies.append(pltpu.make_async_copy(packed, packed_hbm, sems.at[PARTS]))
    copies[PARTS].start()
    sums = narrow(sums)
    part[...] = jnp.broadcast_to(fold(sums, sums), part.shape)
    copy_rows(node_rows, idx_smem, slot_rows)
    emit(slot_rows, count_ref, (s0, s1, s3), own, 2 * comps)
    for copy in copies:
        copy.wait()


def finish_first(factor, prior, total, received, couple, sep_idx, sep_count, parts):
    comps, nodes = factor.shape
    rounds, slots = sep_idx.shape
    f32 = jnp.float32
    packed = (nodes // TILE, 2 * comps, TILE)
    both = jax.ShapeDtypeStruct((4 * comps, slots), jnp.bfloat16)
    return pl.pallas_call(
        first_kernel,
        out_shape=[
            jax.ShapeDtypeStruct((comps, nodes), f32),
            jax.ShapeDtypeStruct(packed, jnp.bfloat16),
            jax.ShapeDtypeStruct((parts, TILE), f32),
            both,
            both,
            both,
            jax.ShapeDtypeStruct((2 * comps, slots), jnp.bfloat16),
        ],
        in_specs=[HBM] * 3 + [VMEM] * 4 + [HBM, SMEM, SMEM],
        out_specs=[HBM, HBM] + [VMEM] * 5,
        scratch_shapes=[
            pltpu.VMEM((nodes, TILE), f32),
            pltpu.VMEM((rounds * slots, TILE), f32),
            pltpu.VMEM((comps, nodes), f32),
            pltpu.VMEM(packed, jnp.bfloat16),
            pltpu.VMEM((comps, nodes), f32),
            pltpu.VMEM((comps, nodes), f32),
            pltpu.VMEM((nodes // TILE, comps, TILE), f32),
            pltpu.VMEM(couple.shape, couple.dtype),
            pltpu.SemaphoreType.DMA((PARTS + 2,)),
            pltpu.SemaphoreType.DMA((3, PARTS)),
        ],
        compiler_params=pltpu.CompilerParams(vmem_limit_bytes=50 * MIB),
        name="finish_first",
    )(factor, prior, total, *received, couple, sep_idx, sep_count)


def beta_of(change, nodes_all):
    return MOMENTUM_CAP * 0.5 * (1.0 + jnp.tanh(change / nodes_all))


def last_kernel(nodes_all, current_hbm, factor_hbm, parts, total_hbm, r0, r1, r2, r3, couple_hbm, idx_smem, count_ref,
                updated_hbm, part, spread, extra_rows, current, updated, factor, total, couple,
                in_sems, out_sems, pair_sem):
    bring = pltpu.make_async_copy(couple_hbm, couple, pair_sem.at[0])
    bring.start()
    come = (
        part_copies(current_hbm, current, in_sems.at[0]),
        part_copies(factor_hbm, factor, in_sems.at[1]),
        block_copies(total_hbm, total, in_sems.at[2]),
    )
    for i in range(PARTS):
        for copies in come:
            copies[i].start()
    comps, nodes = current.shape
    lane = lax.broadcasted_iota(jnp.int32, (1, TILE), 1)
    summed = jnp.sum(parts[...], axis=0, keepdims=True)
    change = jnp.sum(jnp.where(lane < 64, summed, 0.0), axis=1, keepdims=True)
    beta = beta_of(change, nodes_all)
    gap = beta - BETA0
    bring.wait()
    couple_rows(
        r2.shape[0], (r0, r1, r2, r3), couple, count_ref, extra_rows,
        lambda e: e[:comps] + gap * e[comps:],
    )
    scatter_rows(extra_rows, idx_smem, spread)

    def step(c, sums):
        u = current[:, span(c)]
        blend = u + beta * (u - factor[:, span(c)])
        both = wide_total(total, c)
        applied = both[:comps] + gap * both[comps:] + spread[span(c), :].T[:comps]
        moved = blend + applied
        square = jnp.sum(moved * moved, axis=0, keepdims=True)
        new = moved * lax.rsqrt(jnp.maximum(square, 1.0))
        updated[:, span(c)] = new
        return sums[0] + applied * (new - u), sums[1] + applied * new

    zero = jnp.zeros((comps, WIDE * TILE), jnp.float32)
    sums = (zero, zero)
    leave = part_copies(updated, updated_hbm, out_sems)
    each = nodes // (WIDE * TILE * PARTS)
    for i in range(PARTS):
        for arriving in come:
            arriving[i].wait()
        sums = lax.fori_loop(i * each, (i + 1) * each, step, sums, unroll=2)
        leave[i].start()
    part[...] = jnp.broadcast_to(fold(narrow(sums[0]), narrow(sums[1])), part.shape)
    for copy in leave:
        copy.wait()


def finish_last(current, factor, parts, total, received, couple, sep_idx, sep_count, nodes_all):
    comps, nodes = factor.shape
    rounds, slots = sep_idx.shape
    f32 = jnp.float32

    def body(*refs):
        last_kernel(nodes_all, *refs)

    return pl.pallas_call(
        body,
        out_shape=[
            jax.ShapeDtypeStruct((comps, nodes), f32),
            jax.ShapeDtypeStruct(parts.shape, f32),
        ],
        in_specs=[HBM, HBM, VMEM, HBM] + [VMEM] * 4 + [HBM, SMEM, SMEM],
        out_specs=[HBM, VMEM],
        scratch_shapes=[
            pltpu.VMEM((nodes, TILE), f32),
            pltpu.VMEM((rounds * slots, TILE), f32),
            pltpu.VMEM((comps, nodes), f32),
            pltpu.VMEM((comps, nodes), f32),
            pltpu.VMEM((comps, nodes), f32),
            pltpu.VMEM((nodes // TILE, 2 * comps, TILE), f32),
            pltpu.VMEM(couple.shape, couple.dtype),
            pltpu.SemaphoreType.DMA((3, PARTS)),
            pltpu.SemaphoreType.DMA((PARTS,)),
            pltpu.SemaphoreType.DMA((1,)),
        ],
        compiler_params=pltpu.CompilerParams(vmem_limit_bytes=50 * MIB),
        name="finish_last",
    )(current, factor, parts, total, *received, couple, sep_idx, sep_count)


def hop(value, mask, size):
    return lax.ppermute(value, AXES, [(i, i ^ mask) for i in range(size)])


def exchange(sent, branch, source, size):
    own = sent[3]
    rows = own.shape[0]
    got = [hop(value, m, size) for value, m in zip(sent, (size - 1, size // 2, 1))]
    low, top = source[0] & 1, source[0] >= 2
    held = jnp.where(
        top,
        jnp.where(low == 1, got[0][rows:], got[1][rows:]),
        jnp.where(low == 1, got[2][rows:], own),
    )
    branches = [lambda v: v] + [lambda v, m=m: hop(v, 2 * m, size) for m in range(1, size // 4)]
    third = lax.switch(branch[0], branches, held)
    return [got[0], got[1], third, got[2]]


def share(part):
    return lax.all_to_all(part, AXES, 0, 0, tiled=True)


def local(
    factor, prior, tile_src, tile_dst, tile_count, tile_vals, sep_idx, sep_count, couple, masks
):
    size = lax.axis_size(AXES)
    comps, nodes = factor.shape
    nodes_all = size * nodes
    idx, pairs = sep_idx[0], couple[0]
    packed, *sent, branch, source = prepare(masks, factor, prior, idx, sep_count, size)
    received = exchange(sent, branch, source, size)
    total = tile_product(packed, tile_src, tile_dst, tile_count, tile_vals, comps)
    current, packed, part, *sent = finish_first(
        factor, prior, total, received, pairs, idx, sep_count, size
    )
    parts = share(part)
    received = exchange(sent, branch, source, size)
    total = tile_product(packed, tile_src, tile_dst, tile_count, tile_vals, 2 * comps)
    updated, part = finish_last(
        current, factor, parts, total, received, pairs, idx, sep_count, nodes_all
    )
    summed = jnp.sum(share(part), axis=0)
    beta = beta_of(jnp.sum(summed[:64]), nodes_all)
    energy = jnp.sum(summed[64:]) / nodes_all
    return updated, beta, energy


def solution(mesh):
    in_specs = (
        P(None, ("row", "col")),
        P(None, ("row", "col")),
        P(("row", "col"), None),
        P(("row", "col"), None),
        P(("row", "col")),
        P(("row", "col"), None, None),
        P(("row", "col"), None, None),
        P(("row", "col"), None),
        P(("row", "col"), None, None, None),
        P(),
    )
    out_specs = (P(None, ("row", "col")), P(), P())
    return jax.shard_map(local, mesh=mesh, in_specs=in_specs, out_specs=out_specs, check_vma=False)
```

```python
import jax
import jax.numpy as jnp
from jax import lax
from jax.experimental import pallas as pl
from jax.experimental.pallas import tpu as pltpu
from jax.sharding import PartitionSpec as P

TILE = 128
MOMENTUM_CAP = 0.9
BETA0 = 0.5 * MOMENTUM_CAP
AXES = ("row", "col")
MIB = 1024 * 1024
WIDE = 4
BATCH = 16
GROUP = 96
SMEM = pl.BlockSpec(memory_space=pltpu.SMEM)
VMEM = pl.BlockSpec(memory_space=pltpu.VMEM)
HBM = pl.BlockSpec(memory_space=pltpu.HBM)
PARTS = 4


def in_hbm(x):
    return pltpu.with_memory_space_constraint(x, pltpu.HBM)


def in_vmem(x):
    return pltpu.with_memory_space_constraint(x, pltpu.VMEM)


def span(c):
    return pl.ds(pl.multiple_of(c * WIDE * TILE, WIDE * TILE), WIDE * TILE)


def identity(n):
    row = lax.broadcasted_iota(jnp.int32, (n, n), 0)
    return jnp.where(row == lax.broadcasted_iota(jnp.int32, (n, n), 1), 1.0, 0.0).astype(jnp.bfloat16)


def turn_into(rows_ref, c, eye, values):
    n = eye.shape[0]
    for i in range(values.shape[1] // n):
        turned = lax.dot_general(
            eye, values[:, i * n : (i + 1) * n], (((1,), (1,)), ((), ())),
            preferred_element_type=jnp.float32,
        )
        start = pl.multiple_of(c * WIDE * TILE + i * n, n)
        rows_ref[pl.ds(start, n), : values.shape[0]] = turned


def copy_rows(node_rows, idx_smem, slot_rows):
    rounds, slots = idx_smem.shape
    for k in range(rounds):

        def step(c, _, k=k):
            at = [idx_smem[k, c * BATCH + j] for j in range(BATCH)]
            rows = [node_rows[pl.ds(at[j], 1), :] for j in range(BATCH)]
            for j in range(BATCH):
                slot_rows[pl.ds(k * slots + c * BATCH + j, 1), :] = rows[j]
            return 0

        lax.fori_loop(0, slots // BATCH, step, 0, unroll=2)


def columns(slot_rows, k, count_ref, rows, comps, slots):
    got = slot_rows[k * slots : (k + 1) * slots, :].T[:rows]
    keep = lax.broadcasted_iota(jnp.int32, got.shape, 1) < count_ref[0, k]
    if rows > comps:
        keep = keep & (lax.broadcasted_iota(jnp.int32, got.shape, 0) < comps)
    return jnp.where(keep, got, 0.0).astype(jnp.bfloat16)


def emit(slot_rows, count_ref, outs, own, comps):
    rows, slots = own.shape
    shared = columns(slot_rows, 2, count_ref, rows, comps, slots)
    own[...] = shared
    for k, out in zip((0, 1, 3), outs):
        out[:rows] = columns(slot_rows, k, count_ref, rows, comps, slots)
        out[rows:] = shared


def part_copies(source, target, sems):
    width = source.shape[1] // PARTS
    return [
        pltpu.make_async_copy(
            source.at[:, pl.ds(i * width, width)], target.at[:, pl.ds(i * width, width)], sems.at[i]
        )
        for i in range(PARTS)
    ]


def prepare_kernel(size, masks, factor_hbm, prior_hbm, couple_hbm, vals_hbm, idx_smem, count_ref,
                   packed, s0, s1, s3, own, source, branch, factor, start, couple, vals,
                   node_rows, slot_rows, prior, sems, more_sems):
    f_copies = part_copies(factor_hbm, factor, sems.at[0])
    p_copies = part_copies(prior_hbm, prior, sems.at[1])
    for i in range(PARTS):
        f_copies[i].start()
        p_copies[i].start()
    each = vals.shape[0] // PARTS
    brought = [
        pltpu.make_async_copy(
            vals_hbm.at[pl.ds(i * each, each)], vals.at[pl.ds(i * each, each)], more_sems.at[i]
        )
        for i in range(PARTS)
    ]
    brought.append(pltpu.make_async_copy(couple_hbm, couple, more_sems.at[PARTS]))
    comps, nodes = factor.shape
    rows = packed.shape[1]
    mask = masks[2]
    top, bottom = (mask >= size // 2).astype(jnp.int32), mask & 1
    source[0] = 2 * top + bottom
    rest = jnp.where(top + bottom == 2, mask ^ (size - 1), mask)
    branch[0] = lax.shift_right_logical(rest & (size // 2 - 1), 1)
    pad = jnp.zeros((rows - comps, WIDE * TILE), jnp.float32)
    eye = identity(2 * TILE)

    def step(c, _):
        f = factor[:, span(c)]
        blend = f + BETA0 * (f - prior[:, span(c)])
        start[:, span(c)] = blend
        values = jnp.concatenate([blend, pad], axis=0).astype(packed.dtype)
        turn_into(node_rows, c, eye, values)
        for i in range(WIDE):
            packed[c * WIDE + i] = values[:, i * TILE : (i + 1) * TILE]
        return 0

    each = nodes // (WIDE * TILE * PARTS)
    for i in range(PARTS):
        f_copies[i].wait()
        p_copies[i].wait()
        if i == 0:
            for copy in brought:
                copy.start()
        lax.fori_loop(i * each, (i + 1) * each, step, 0, unroll=2)
    copy_rows(node_rows, idx_smem, slot_rows)
    emit(slot_rows, count_ref, (s0, s1, s3), own, comps)
    for copy in brought:
        copy.wait()


def prepare(masks, factor, prior, couple, tile_vals, sep_idx, sep_count, size):
    comps, nodes = factor.shape
    rounds, slots = sep_idx.shape
    rows = 32

    def body(*refs):
        prepare_kernel(size, *refs)

    both = jax.ShapeDtypeStruct((2 * rows, slots), jnp.bfloat16)
    return pl.pallas_call(
        body,
        out_shape=[
            pltpu.VMEM((nodes // TILE, rows, TILE), jnp.bfloat16),
            both,
            both,
            both,
            jax.ShapeDtypeStruct((rows, slots), jnp.bfloat16),
            jax.ShapeDtypeStruct((1,), jnp.int32),
            jax.ShapeDtypeStruct((1,), jnp.int32),
            pltpu.VMEM((comps, nodes), jnp.float32),
            pltpu.VMEM((comps, nodes), jnp.float32),
            pltpu.VMEM(couple.shape, couple.dtype),
            pltpu.VMEM(tile_vals.shape, tile_vals.dtype),
        ],
        in_specs=[SMEM] + [HBM] * 4 + [SMEM, SMEM],
        out_specs=[VMEM] * 5 + [SMEM] * 2 + [VMEM] * 4,
        scratch_shapes=[
            pltpu.VMEM((nodes, TILE), jnp.float32),
            pltpu.VMEM((rounds * slots, TILE), jnp.float32),
            pltpu.VMEM((comps, nodes), jnp.float32),
            pltpu.SemaphoreType.DMA((2, PARTS)),
            pltpu.SemaphoreType.DMA((PARTS + 1,)),
        ],
        compiler_params=pltpu.CompilerParams(vmem_limit_bytes=20 * MIB),
        name="prepare",
    )(
        in_hbm(masks), in_hbm(factor), in_hbm(prior), in_hbm(couple), in_hbm(tile_vals),
        in_hbm(sep_idx), in_hbm(sep_count),
    )


def tile_steps(keep, group, arrive, src, dst, count, packed, vals, total):
    spare, rows, _ = packed.shape

    def one(g, _):
        arrive(g)
        base = g * group
        products = []
        for j in range(0, group, 2):
            left = jnp.concatenate([packed[src[0, base + j]], packed[src[0, base + j + 1]]], axis=0)
            right = jnp.concatenate([vals[base + j], vals[base + j + 1]], axis=1)
            both = jnp.dot(left, right, preferred_element_type=jnp.float32)
            products += [both[:keep, :TILE], both[rows : rows + keep, TILE:]]
        for j in range(group):
            to = jnp.where(base + j < count[0, 0], dst[0, base + j], spare)
            total[to] += products[j]
        return 0

    lax.fori_loop(0, vals.shape[0] // group, one, 0)


def resident_kernel(keep, group, src, dst, count, packed, vals, total):
    total[...] = jnp.zeros_like(total)
    tile_steps(keep, group, lambda g: None, src, dst, count, packed, vals, total)


def streamed_kernel(keep, group, src, dst, count, packed_hbm, vals_hbm, total, packed, vals, sems):
    groups = vals.shape[0] // group
    bring = pltpu.make_async_copy(packed_hbm, packed, sems.at[groups])
    bring.start()

    def tiles(g):
        at = pl.ds(g * group, group)
        return pltpu.make_async_copy(vals_hbm.at[at], vals.at[at], sems.at[g])

    for g in range(groups):
        tiles(g).start()
    total[...] = jnp.zeros_like(total)
    bring.wait()
    tile_steps(keep, group, lambda g: tiles(g).wait(), src, dst, count, packed, vals, total)


def tile_product(packed, tile_src, tile_dst, tile_count, tile_vals, keep, resident):
    blocks, rows, _ = packed.shape
    slots = tile_vals.shape[0]
    group = GROUP if resident else 64

    def body(*refs):
        (resident_kernel if resident else streamed_kernel)(keep, group, *refs)

    place, spec = (in_vmem, VMEM) if resident else (in_hbm, HBM)
    scratch = [
        pltpu.VMEM(packed.shape, packed.dtype),
        pltpu.VMEM(tile_vals.shape, tile_vals.dtype),
        pltpu.SemaphoreType.DMA((slots // group + 1,)),
    ]
    return pl.pallas_call(
        body,
        out_shape=pltpu.VMEM((blocks + 1, keep, TILE), jnp.float32),
        in_specs=[SMEM, SMEM, SMEM, spec, spec],
        out_specs=VMEM,
        scratch_shapes=[] if resident else scratch,
        compiler_params=pltpu.CompilerParams(vmem_limit_bytes=(8 if resident else 24) * MIB),
        cost_estimate=pl.CostEstimate(
            flops=2 * slots * rows * TILE * TILE,
            bytes_accessed=slots * TILE * TILE * 2 + blocks * rows * TILE * 8,
            transcendentals=0,
        ),
        name="tile_product",
    )(tile_src, tile_dst, tile_count, place(packed), place(tile_vals))


def scatter_rows(extra_rows, idx_smem, spread):
    rounds, slots = idx_smem.shape
    spread[...] = jnp.zeros_like(spread)
    for k in range(rounds):

        def step(c, _, k=k):
            at = [idx_smem[k, c * BATCH + j] for j in range(BATCH)]
            new = [
                spread[pl.ds(at[j], 1), :] + extra_rows[pl.ds(k * slots + c * BATCH + j, 1), :]
                for j in range(BATCH)
            ]
            for j in range(BATCH):
                spread[pl.ds(at[j], 1), :] = new[j]
            return 0

        lax.fori_loop(0, slots // BATCH, step, 0, unroll=2)


def couple_rows(rows, received, couple, count_ref, extra_rows, combine):
    for k, ref in enumerate(received):
        slots = ref.shape[1]
        extra = combine(jnp.dot(ref[:rows], couple[k], preferred_element_type=jnp.float32))
        slot = lax.broadcasted_iota(jnp.int32, extra.shape, 1)
        extra = jnp.where(slot < count_ref[0, k], extra, 0.0)
        fill = jnp.zeros((TILE - extra.shape[0], slots), jnp.float32)
        extra_rows[k * slots : (k + 1) * slots, :] = jnp.concatenate([extra, fill], axis=0).T


def wide_total(total, c):
    return jnp.concatenate([total[c * WIDE + i] for i in range(WIDE)], axis=1)


def narrow(sums):
    return sum(sums[:, i * TILE : (i + 1) * TILE] for i in range(WIDE))


def fold(change, total):
    a = jnp.sum(change, axis=0, keepdims=True)
    b = jnp.sum(total, axis=0, keepdims=True)
    a = a + pltpu.roll(a, 64, 1)
    b = b + pltpu.roll(b, 64, 1)
    lane = lax.broadcasted_iota(jnp.int32, a.shape, 1)
    return jnp.where(lane < 64, a, b)


def first_kernel(factor, start, total, r0, r1, r2, r3, couple, idx_smem, count_ref,
                 updated_hbm, packed_hbm, part, s0, s1, s3, own, node_rows, slot_rows, updated, packed, sems):
    comps, nodes = factor.shape
    couple_rows(r2.shape[0], (r0, r1, r2, r3), couple, count_ref, slot_rows, lambda e: e[:comps])
    scatter_rows(slot_rows, idx_smem, node_rows)
    eye = identity(2 * TILE)

    def step(c, sums):
        f = factor[:, span(c)]
        blend = start[:, span(c)]
        applied = wide_total(total, c) + node_rows[span(c), :].T[:comps]
        moved = blend + applied
        square = jnp.sum(moved * moved, axis=0, keepdims=True)
        u = moved * lax.rsqrt(jnp.maximum(square, 1.0))
        d = u - f
        updated[:, span(c)] = u
        both = jnp.concatenate([u + BETA0 * d, d], axis=0).astype(packed.dtype)
        turn_into(node_rows, c, eye, both)
        for i in range(WIDE):
            packed[c * WIDE + i] = both[:, i * TILE : (i + 1) * TILE]
        return sums + applied * d

    copies = part_copies(updated, updated_hbm, sems)
    sums = jnp.zeros((comps, WIDE * TILE), jnp.float32)
    each = nodes // (WIDE * TILE * PARTS)
    for i in range(PARTS):
        sums = lax.fori_loop(i * each, (i + 1) * each, step, sums, unroll=2)
        copies[i].start()
    copies.append(pltpu.make_async_copy(packed, packed_hbm, sems.at[PARTS]))
    copies[PARTS].start()
    sums = narrow(sums)
    part[...] = jnp.broadcast_to(fold(sums, sums), part.shape)
    copy_rows(node_rows, idx_smem, slot_rows)
    emit(slot_rows, count_ref, (s0, s1, s3), own, 2 * comps)
    for copy in copies:
        copy.wait()


def finish_first(factor, start, total, received, couple, sep_idx, sep_count, parts):
    comps, nodes = factor.shape
    rounds, slots = sep_idx.shape
    f32 = jnp.float32
    packed = (nodes // TILE, 2 * comps, TILE)
    both = jax.ShapeDtypeStruct((4 * comps, slots), jnp.bfloat16)
    return pl.pallas_call(
        first_kernel,
        out_shape=[
            pltpu.HBM((comps, nodes), f32),
            pltpu.HBM(packed, jnp.bfloat16),
            jax.ShapeDtypeStruct((parts, TILE), f32),
            both,
            both,
            both,
            jax.ShapeDtypeStruct((2 * comps, slots), jnp.bfloat16),
        ],
        in_specs=[VMEM] * 8 + [SMEM, SMEM],
        out_specs=[HBM, HBM] + [VMEM] * 5,
        scratch_shapes=[
            pltpu.VMEM((nodes, TILE), f32),
            pltpu.VMEM((rounds * slots, TILE), f32),
            pltpu.VMEM((comps, nodes), f32),
            pltpu.VMEM(packed, jnp.bfloat16),
            pltpu.SemaphoreType.DMA((PARTS + 1,)),
        ],
        compiler_params=pltpu.CompilerParams(vmem_limit_bytes=16 * MIB),
        name="finish_first",
    )(
        in_vmem(factor), in_vmem(start), in_vmem(total), *received, in_vmem(couple), sep_idx, sep_count
    )


def beta_of(change, nodes_all):
    return MOMENTUM_CAP * 0.5 * (1.0 + jnp.tanh(change / nodes_all))


def last_kernel(nodes_all, current_hbm, factor, parts, total, r0, r1, r2, r3, couple, idx_smem, count_ref,
                updated_hbm, part, spread, extra_rows, current, updated, in_sems, sems):
    come = part_copies(current_hbm, current, in_sems)
    for copy in come:
        copy.start()
    comps, nodes = current.shape
    lane = lax.broadcasted_iota(jnp.int32, (1, TILE), 1)
    summed = jnp.sum(parts[...], axis=0, keepdims=True)
    change = jnp.sum(jnp.where(lane < 64, summed, 0.0), axis=1, keepdims=True)
    beta = beta_of(change, nodes_all)
    gap = beta - BETA0
    couple_rows(
        r2.shape[0], (r0, r1, r2, r3), couple, count_ref, extra_rows,
        lambda e: e[:comps] + gap * e[comps:],
    )
    scatter_rows(extra_rows, idx_smem, spread)

    def step(c, sums):
        u = current[:, span(c)]
        blend = u + beta * (u - factor[:, span(c)])
        both = wide_total(total, c)
        applied = both[:comps] + gap * both[comps:] + spread[span(c), :].T[:comps]
        moved = blend + applied
        square = jnp.sum(moved * moved, axis=0, keepdims=True)
        new = moved * lax.rsqrt(jnp.maximum(square, 1.0))
        updated[:, span(c)] = new
        return sums[0] + applied * (new - u), sums[1] + applied * new

    zero = jnp.zeros((comps, WIDE * TILE), jnp.float32)
    sums = (zero, zero)
    leave = part_copies(updated, updated_hbm, sems)
    each = nodes // (WIDE * TILE * PARTS)
    for i in range(PARTS):
        come[i].wait()
        sums = lax.fori_loop(i * each, (i + 1) * each, step, sums, unroll=2)
        leave[i].start()
    part[...] = jnp.broadcast_to(fold(narrow(sums[0]), narrow(sums[1])), part.shape)
    for copy in leave:
        copy.wait()


def finish_last(current, factor, parts, total, received, couple, sep_idx, sep_count, nodes_all):
    comps, nodes = factor.shape
    rounds, slots = sep_idx.shape
    f32 = jnp.float32

    def body(*refs):
        last_kernel(nodes_all, *refs)

    return pl.pallas_call(
        body,
        out_shape=[
            pltpu.HBM((comps, nodes), f32),
            jax.ShapeDtypeStruct(parts.shape, f32),
        ],
        in_specs=[HBM] + [VMEM] * 8 + [SMEM, SMEM],
        out_specs=[HBM, VMEM],
        scratch_shapes=[
            pltpu.VMEM((nodes, TILE), f32),
            pltpu.VMEM((rounds * slots, TILE), f32),
            pltpu.VMEM((comps, nodes), f32),
            pltpu.VMEM((comps, nodes), f32),
            pltpu.SemaphoreType.DMA((PARTS,)),
            pltpu.SemaphoreType.DMA((PARTS,)),
        ],
        compiler_params=pltpu.CompilerParams(vmem_limit_bytes=16 * MIB),
        name="finish_last",
    )(
        in_hbm(current), in_vmem(factor), parts, in_vmem(total), *received, in_vmem(couple), sep_idx, sep_count
    )


def hop(value, mask, size):
    return lax.ppermute(value, AXES, [(i, i ^ mask) for i in range(size)])


def choose_kernel(source, own, low, high, both, held):
    rows = own.shape[0]
    s = source[0]

    @pl.when(s == 0)
    def _():
        held[...] = own[...]

    for i, ref in enumerate((low, high, both)):

        @pl.when(s == i + 1)
        def _(ref=ref):
            held[...] = ref[rows:]


def choose(source, own, low, high, both):
    return pl.pallas_call(
        choose_kernel,
        out_shape=jax.ShapeDtypeStruct(own.shape, own.dtype),
        in_specs=[SMEM] + [VMEM] * 4,
        out_specs=VMEM,
        compiler_params=pltpu.CompilerParams(vmem_limit_bytes=2 * MIB),
        name="choose",
    )(source, own, low, high, both)


def exchange(sent, branch, source, size):
    own = sent[3]
    rows = own.shape[0]
    got = [hop(value, m, size) for value, m in zip(sent, (size - 1, size // 2, 1))]
    held = choose(source, own, got[2], got[1], got[0])
    branches = [lambda v: v] + [lambda v, m=m: hop(v, 2 * m, size) for m in range(1, size // 4)]
    third = lax.switch(branch[0], branches, held)
    return [got[0], got[1], third, got[2]]


def share(part):
    return lax.all_to_all(part, AXES, 0, 0, tiled=True)


def local(
    factor, prior, tile_src, tile_dst, tile_count, tile_vals, sep_idx, sep_count, couple, masks
):
    size = lax.axis_size(AXES)
    comps, nodes = factor.shape
    nodes_all = size * nodes
    idx, pairs = sep_idx[0], couple[0]
    live = tile_count.reshape(1, 1)
    packed, s0, s1, s3, own, source, branch, factor, start, pairs, vals = prepare(
        masks, factor, prior, pairs, tile_vals, idx, sep_count, size
    )
    received = exchange([s0, s1, s3, own], branch, source, size)
    total = tile_product(packed, tile_src, tile_dst, live, vals, comps, True)
    current, packed, part, *sent = finish_first(
        factor, start, total, received, pairs, idx, sep_count, size
    )
    parts = share(part)
    received = exchange(sent, branch, source, size)
    total = tile_product(packed, tile_src, tile_dst, live, tile_vals, 2 * comps, False)
    updated, part = finish_last(
        current, factor, parts, total, received, pairs, idx, sep_count, nodes_all
    )
    summed = jnp.sum(share(part), axis=0)
    beta = beta_of(jnp.sum(summed[:64]), nodes_all)
    energy = jnp.sum(summed[64:]) / nodes_all
    return updated, beta, energy


def solution(mesh):
    in_specs = (
        P(None, ("row", "col")),
        P(None, ("row", "col")),
        P(("row", "col"), None),
        P(("row", "col"), None),
        P(("row", "col")),
        P(("row", "col"), None, None),
        P(("row", "col"), None, None),
        P(("row", "col"), None),
        P(("row", "col"), None, None, None),
        P(),
    )
    out_specs = (P(None, ("row", "col")), P(), P())
    return jax.shard_map(local, mesh=mesh, in_specs=in_specs, out_specs=out_specs, check_vma=False)
```

```python
import jax
import jax.numpy as jnp
from jax import lax
from jax.experimental import pallas as pl
from jax.experimental.pallas import tpu as pltpu
from jax.sharding import PartitionSpec as P

TILE = 128
MOMENTUM_CAP = 0.9
BETA0 = 0.5 * MOMENTUM_CAP
AXES = ("row", "col")
MIB = 1024 * 1024
WIDE = 4
BATCH = 16
STRETCH_BITS = 5
STRETCH = 1 << STRETCH_BITS
GROUP = 96
SMEM = pl.BlockSpec(memory_space=pltpu.SMEM)
VMEM = pl.BlockSpec(memory_space=pltpu.VMEM)
HBM = pl.BlockSpec(memory_space=pltpu.HBM)
PARTS = 4


def in_hbm(x):
    return pltpu.with_memory_space_constraint(x, pltpu.HBM)


def in_vmem(x):
    return pltpu.with_memory_space_constraint(x, pltpu.VMEM)


def span(c):
    return pl.ds(pl.multiple_of(c * WIDE * TILE, WIDE * TILE), WIDE * TILE)


def identity(n):
    row = lax.broadcasted_iota(jnp.int32, (n, n), 0)
    return jnp.where(row == lax.broadcasted_iota(jnp.int32, (n, n), 1), 1.0, 0.0).astype(jnp.bfloat16)


def turn_into(rows_ref, c, eye, values):
    n = eye.shape[0]
    for i in range(values.shape[1] // n):
        turned = lax.dot_general(
            eye, values[:, i * n : (i + 1) * n], (((1,), (1,)), ((), ())),
            preferred_element_type=jnp.float32,
        )
        start = pl.multiple_of(c * WIDE * TILE + i * n, n)
        rows_ref[pl.ds(start, n), : values.shape[0]] = turned


def over_live(slots, live, body):
    def step(c, _):
        body(pl.multiple_of(c * STRETCH, STRETCH))
        return 0

    lax.fori_loop(0, jnp.minimum(lax.shift_right_logical(live + STRETCH - 1, STRETCH_BITS), slots // STRETCH), step, 0)


def copy_rows(node_rows, idx_smem, count_ref, slot_rows):
    rounds, slots = idx_smem.shape
    for k in range(rounds):

        def body(first, k=k):
            for q in range(0, STRETCH, BATCH):
                at = [idx_smem[k, first + q + j] for j in range(BATCH)]
                rows = [node_rows[pl.ds(at[j], 1), :] for j in range(BATCH)]
                for j in range(BATCH):
                    slot_rows[pl.ds(k * slots + first + q + j, 1), :] = rows[j]

        over_live(slots, count_ref[0, k], body)


def columns(slot_rows, k, count_ref, rows, comps, slots):
    got = slot_rows[k * slots : (k + 1) * slots, :].T[:rows]
    keep = lax.broadcasted_iota(jnp.int32, got.shape, 1) < count_ref[0, k]
    if rows > comps:
        keep = keep & (lax.broadcasted_iota(jnp.int32, got.shape, 0) < comps)
    return jnp.where(keep, got, 0.0).astype(jnp.bfloat16)


def emit(slot_rows, count_ref, outs, own, comps):
    rows, slots = own.shape
    shared = columns(slot_rows, 2, count_ref, rows, comps, slots)
    own[...] = shared
    for k, out in zip((0, 1, 3), outs):
        out[:rows] = columns(slot_rows, k, count_ref, rows, comps, slots)
        out[rows:] = shared


def part_copies(source, target, sems):
    width = source.shape[1] // PARTS
    return [
        pltpu.make_async_copy(
            source.at[:, pl.ds(i * width, width)], target.at[:, pl.ds(i * width, width)], sems.at[i]
        )
        for i in range(PARTS)
    ]


def prepare_kernel(size, masks, factor_hbm, prior_hbm, couple_hbm, vals_hbm, idx_smem, count_ref,
                   packed, s0, s1, s3, own, source, branch, factor, start, couple, vals,
                   node_rows, slot_rows, prior, sems, more_sems):
    f_copies = part_copies(factor_hbm, factor, sems.at[0])
    p_copies = part_copies(prior_hbm, prior, sems.at[1])
    for i in range(PARTS):
        f_copies[i].start()
        p_copies[i].start()
    each = vals.shape[0] // PARTS
    brought = [
        pltpu.make_async_copy(
            vals_hbm.at[pl.ds(i * each, each)], vals.at[pl.ds(i * each, each)], more_sems.at[i]
        )
        for i in range(PARTS)
    ]
    brought.append(pltpu.make_async_copy(couple_hbm, couple, more_sems.at[PARTS]))
    comps, nodes = factor.shape
    rows = packed.shape[1]
    mask = masks[2]
    top, bottom = (mask >= size // 2).astype(jnp.int32), mask & 1
    source[0] = 2 * top + bottom
    rest = jnp.where(top + bottom == 2, mask ^ (size - 1), mask)
    branch[0] = lax.shift_right_logical(rest & (size // 2 - 1), 1)
    pad = jnp.zeros((rows - comps, WIDE * TILE), jnp.float32)
    eye = identity(2 * TILE)

    def step(c, _):
        f = factor[:, span(c)]
        blend = f + BETA0 * (f - prior[:, span(c)])
        start[:, span(c)] = blend
        values = jnp.concatenate([blend, pad], axis=0).astype(packed.dtype)
        turn_into(node_rows, c, eye, values)
        for i in range(WIDE):
            packed[c * WIDE + i] = values[:, i * TILE : (i + 1) * TILE]
        return 0

    each = nodes // (WIDE * TILE * PARTS)
    for i in range(PARTS):
        f_copies[i].wait()
        p_copies[i].wait()
        if i == 0:
            for copy in brought:
                copy.start()
        lax.fori_loop(i * each, (i + 1) * each, step, 0, unroll=2)
    copy_rows(node_rows, idx_smem, count_ref, slot_rows)
    emit(slot_rows, count_ref, (s0, s1, s3), own, comps)
    for copy in brought:
        copy.wait()


def prepare(masks, factor, prior, couple, tile_vals, sep_idx, sep_count, size):
    comps, nodes = factor.shape
    rounds, slots = sep_idx.shape
    rows = 32

    def body(*refs):
        prepare_kernel(size, *refs)

    both = jax.ShapeDtypeStruct((2 * rows, slots), jnp.bfloat16)
    return pl.pallas_call(
        body,
        out_shape=[
            pltpu.VMEM((nodes // TILE, rows, TILE), jnp.bfloat16),
            both,
            both,
            both,
            jax.ShapeDtypeStruct((rows, slots), jnp.bfloat16),
            jax.ShapeDtypeStruct((1,), jnp.int32),
            jax.ShapeDtypeStruct((1,), jnp.int32),
            pltpu.VMEM((comps, nodes), jnp.float32),
            pltpu.VMEM((comps, nodes), jnp.float32),
            pltpu.VMEM(couple.shape, couple.dtype),
            pltpu.VMEM(tile_vals.shape, tile_vals.dtype),
        ],
        in_specs=[SMEM] + [HBM] * 4 + [SMEM, SMEM],
        out_specs=[VMEM] * 5 + [SMEM] * 2 + [VMEM] * 4,
        scratch_shapes=[
            pltpu.VMEM((nodes, TILE), jnp.float32),
            pltpu.VMEM((rounds * slots, TILE), jnp.float32),
            pltpu.VMEM((comps, nodes), jnp.float32),
            pltpu.SemaphoreType.DMA((2, PARTS)),
            pltpu.SemaphoreType.DMA((PARTS + 1,)),
        ],
        compiler_params=pltpu.CompilerParams(vmem_limit_bytes=20 * MIB),
        name="prepare",
    )(
        in_hbm(masks), in_hbm(factor), in_hbm(prior), in_hbm(couple), in_hbm(tile_vals),
        in_hbm(sep_idx), in_hbm(sep_count),
    )


def tile_steps(keep, group, arrive, src, dst, count, packed, vals, total):
    spare, rows, _ = packed.shape

    def one(g, _):
        arrive(g)
        base = g * group
        products = []
        for j in range(0, group, 2):
            left = jnp.concatenate([packed[src[0, base + j]], packed[src[0, base + j + 1]]], axis=0)
            right = jnp.concatenate([vals[base + j], vals[base + j + 1]], axis=1)
            both = jnp.dot(left, right, preferred_element_type=jnp.float32)
            products += [both[:keep, :TILE], both[rows : rows + keep, TILE:]]
        for j in range(group):
            to = jnp.where(base + j < count[0, 0], dst[0, base + j], spare)
            total[to] += products[j]
        return 0

    lax.fori_loop(0, vals.shape[0] // group, one, 0)


def resident_kernel(keep, group, src, dst, count, packed, vals, total):
    total[...] = jnp.zeros_like(total)
    tile_steps(keep, group, lambda g: None, src, dst, count, packed, vals, total)


def streamed_kernel(keep, group, src, dst, count, packed_hbm, vals_hbm, total, packed, vals, sems):
    groups = vals.shape[0] // group
    bring = pltpu.make_async_copy(packed_hbm, packed, sems.at[groups])
    bring.start()

    def tiles(g):
        at = pl.ds(g * group, group)
        return pltpu.make_async_copy(vals_hbm.at[at], vals.at[at], sems.at[g])

    for g in range(groups):
        tiles(g).start()
    total[...] = jnp.zeros_like(total)
    bring.wait()
    tile_steps(keep, group, lambda g: tiles(g).wait(), src, dst, count, packed, vals, total)


def tile_product(packed, tile_src, tile_dst, tile_count, tile_vals, keep, resident):
    blocks, rows, _ = packed.shape
    slots = tile_vals.shape[0]
    group = GROUP if resident else 64

    def body(*refs):
        (resident_kernel if resident else streamed_kernel)(keep, group, *refs)

    place, spec = (in_vmem, VMEM) if resident else (in_hbm, HBM)
    scratch = [
        pltpu.VMEM(packed.shape, packed.dtype),
        pltpu.VMEM(tile_vals.shape, tile_vals.dtype),
        pltpu.SemaphoreType.DMA((slots // group + 1,)),
    ]
    return pl.pallas_call(
        body,
        out_shape=pltpu.VMEM((blocks + 1, keep, TILE), jnp.float32),
        in_specs=[SMEM, SMEM, SMEM, spec, spec],
        out_specs=VMEM,
        scratch_shapes=[] if resident else scratch,
        compiler_params=pltpu.CompilerParams(vmem_limit_bytes=(8 if resident else 24) * MIB),
        cost_estimate=pl.CostEstimate(
            flops=2 * slots * rows * TILE * TILE,
            bytes_accessed=slots * TILE * TILE * 2 + blocks * rows * TILE * 8,
            transcendentals=0,
        ),
        name="tile_product",
    )(tile_src, tile_dst, tile_count, place(packed), place(tile_vals))


def scatter_rows(extra_rows, idx_smem, count_ref, spread):
    rounds, slots = idx_smem.shape
    spread[...] = jnp.zeros_like(spread)
    for k in range(rounds):

        def body(first, k=k):
            for q in range(0, STRETCH, BATCH):
                at = [idx_smem[k, first + q + j] for j in range(BATCH)]
                new = [
                    spread[pl.ds(at[j], 1), :] + extra_rows[pl.ds(k * slots + first + q + j, 1), :]
                    for j in range(BATCH)
                ]
                for j in range(BATCH):
                    spread[pl.ds(at[j], 1), :] = new[j]

        over_live(slots, count_ref[0, k], body)


def couple_rows(rows, received, couple, count_ref, extra_rows, combine):
    for k, ref in enumerate(received):
        slots = ref.shape[1]
        extra = combine(jnp.dot(ref[:rows], couple[k], preferred_element_type=jnp.float32))
        slot = lax.broadcasted_iota(jnp.int32, extra.shape, 1)
        extra = jnp.where(slot < count_ref[0, k], extra, 0.0)
        fill = jnp.zeros((TILE - extra.shape[0], slots), jnp.float32)
        extra_rows[k * slots : (k + 1) * slots, :] = jnp.concatenate([extra, fill], axis=0).T


def wide_total(total, c):
    return jnp.concatenate([total[c * WIDE + i] for i in range(WIDE)], axis=1)


def narrow(sums):
    return sum(sums[:, i * TILE : (i + 1) * TILE] for i in range(WIDE))


def fold(change, total):
    a = jnp.sum(change, axis=0, keepdims=True)
    b = jnp.sum(total, axis=0, keepdims=True)
    a = a + pltpu.roll(a, 64, 1)
    b = b + pltpu.roll(b, 64, 1)
    lane = lax.broadcasted_iota(jnp.int32, a.shape, 1)
    return jnp.where(lane < 64, a, b)


def first_kernel(factor, start, total, r0, r1, r2, r3, couple, idx_smem, count_ref,
                 updated_hbm, packed_hbm, part, s0, s1, s3, own, node_rows, slot_rows, updated, packed, sems):
    comps, nodes = factor.shape
    couple_rows(r2.shape[0], (r0, r1, r2, r3), couple, count_ref, slot_rows, lambda e: e[:comps])
    scatter_rows(slot_rows, idx_smem, count_ref, node_rows)
    eye = identity(2 * TILE)

    def step(c, sums):
        f = factor[:, span(c)]
        blend = start[:, span(c)]
        applied = wide_total(total, c) + node_rows[span(c), :].T[:comps]
        moved = blend + applied
        square = jnp.sum(moved * moved, axis=0, keepdims=True)
        u = moved * lax.rsqrt(jnp.maximum(square, 1.0))
        d = u - f
        updated[:, span(c)] = u
        both = jnp.concatenate([u + BETA0 * d, d], axis=0).astype(packed.dtype)
        turn_into(node_rows, c, eye, both)
        for i in range(WIDE):
            packed[c * WIDE + i] = both[:, i * TILE : (i + 1) * TILE]
        return sums + applied * d

    copies = part_copies(updated, updated_hbm, sems)
    sums = jnp.zeros((comps, WIDE * TILE), jnp.float32)
    each = nodes // (WIDE * TILE * PARTS)
    for i in range(PARTS):
        sums = lax.fori_loop(i * each, (i + 1) * each, step, sums, unroll=2)
        copies[i].start()
    copies.append(pltpu.make_async_copy(packed, packed_hbm, sems.at[PARTS]))
    copies[PARTS].start()
    sums = narrow(sums)
    part[...] = jnp.broadcast_to(fold(sums, sums), part.shape)
    copy_rows(node_rows, idx_smem, count_ref, slot_rows)
    emit(slot_rows, count_ref, (s0, s1, s3), own, 2 * comps)
    for copy in copies:
        copy.wait()


def finish_first(factor, start, total, received, couple, sep_idx, sep_count, parts):
    comps, nodes = factor.shape
    rounds, slots = sep_idx.shape
    f32 = jnp.float32
    packed = (nodes // TILE, 2 * comps, TILE)
    both = jax.ShapeDtypeStruct((4 * comps, slots), jnp.bfloat16)
    return pl.pallas_call(
        first_kernel,
        out_shape=[
            pltpu.HBM((comps, nodes), f32),
            pltpu.HBM(packed, jnp.bfloat16),
            jax.ShapeDtypeStruct((parts, TILE), f32),
            both,
            both,
            both,
            jax.ShapeDtypeStruct((2 * comps, slots), jnp.bfloat16),
        ],
        in_specs=[VMEM] * 8 + [SMEM, SMEM],
        out_specs=[HBM, HBM] + [VMEM] * 5,
        scratch_shapes=[
            pltpu.VMEM((nodes, TILE), f32),
            pltpu.VMEM((rounds * slots, TILE), f32),
            pltpu.VMEM((comps, nodes), f32),
            pltpu.VMEM(packed, jnp.bfloat16),
            pltpu.SemaphoreType.DMA((PARTS + 1,)),
        ],
        compiler_params=pltpu.CompilerParams(vmem_limit_bytes=16 * MIB),
        name="finish_first",
    )(
        in_vmem(factor), in_vmem(start), in_vmem(total), *received, in_vmem(couple), sep_idx, sep_count
    )


def beta_of(change, nodes_all):
    return MOMENTUM_CAP * 0.5 * (1.0 + jnp.tanh(change / nodes_all))


def last_kernel(nodes_all, current_hbm, factor, parts, total, r0, r1, r2, r3, couple, idx_smem, count_ref,
                updated_hbm, part, spread, extra_rows, current, updated, in_sems, sems):
    come = part_copies(current_hbm, current, in_sems)
    for copy in come:
        copy.start()
    comps, nodes = current.shape
    lane = lax.broadcasted_iota(jnp.int32, (1, TILE), 1)
    summed = jnp.sum(parts[...], axis=0, keepdims=True)
    change = jnp.sum(jnp.where(lane < 64, summed, 0.0), axis=1, keepdims=True)
    beta = beta_of(change, nodes_all)
    gap = beta - BETA0
    couple_rows(
        r2.shape[0], (r0, r1, r2, r3), couple, count_ref, extra_rows,
        lambda e: e[:comps] + gap * e[comps:],
    )
    scatter_rows(extra_rows, idx_smem, count_ref, spread)

    def step(c, sums):
        u = current[:, span(c)]
        blend = u + beta * (u - factor[:, span(c)])
        both = wide_total(total, c)
        applied = both[:comps] + gap * both[comps:] + spread[span(c), :].T[:comps]
        moved = blend + applied
        square = jnp.sum(moved * moved, axis=0, keepdims=True)
        new = moved * lax.rsqrt(jnp.maximum(square, 1.0))
        updated[:, span(c)] = new
        return sums[0] + applied * (new - u), sums[1] + applied * new

    zero = jnp.zeros((comps, WIDE * TILE), jnp.float32)
    sums = (zero, zero)
    leave = part_copies(updated, updated_hbm, sems)
    each = nodes // (WIDE * TILE * PARTS)
    for i in range(PARTS):
        come[i].wait()
        sums = lax.fori_loop(i * each, (i + 1) * each, step, sums, unroll=2)
        leave[i].start()
    part[...] = jnp.broadcast_to(fold(narrow(sums[0]), narrow(sums[1])), part.shape)
    for copy in leave:
        copy.wait()


def close_kernel(nodes_all, parts, momentum, energy):
    lane = lax.broadcasted_iota(jnp.int32, (1, TILE), 1)
    summed = jnp.sum(parts[...], axis=0, keepdims=True)
    change = jnp.sum(jnp.where(lane < 64, summed, 0.0), axis=1, keepdims=True)
    total = jnp.sum(jnp.where(lane < 64, 0.0, summed), axis=1, keepdims=True)
    momentum[0] = beta_of(change, nodes_all)[0, 0]
    energy[0] = (total / nodes_all)[0, 0]


def close(parts, nodes_all):
    def body(*refs):
        close_kernel(nodes_all, *refs)

    one = jax.ShapeDtypeStruct((1,), jnp.float32)
    momentum, energy = pl.pallas_call(
        body,
        out_shape=[one, one],
        in_specs=[VMEM],
        out_specs=[SMEM, SMEM],
        compiler_params=pltpu.CompilerParams(vmem_limit_bytes=2 * MIB),
        name="close",
    )(parts)
    return momentum.reshape(()), energy.reshape(())


def finish_last(current, factor, parts, total, received, couple, sep_idx, sep_count, nodes_all):
    comps, nodes = factor.shape
    rounds, slots = sep_idx.shape
    f32 = jnp.float32

    def body(*refs):
        last_kernel(nodes_all, *refs)

    return pl.pallas_call(
        body,
        out_shape=[
            pltpu.HBM((comps, nodes), f32),
            jax.ShapeDtypeStruct(parts.shape, f32),
        ],
        in_specs=[HBM] + [VMEM] * 8 + [SMEM, SMEM],
        out_specs=[HBM, VMEM],
        scratch_shapes=[
            pltpu.VMEM((nodes, TILE), f32),
            pltpu.VMEM((rounds * slots, TILE), f32),
            pltpu.VMEM((comps, nodes), f32),
            pltpu.VMEM((comps, nodes), f32),
            pltpu.SemaphoreType.DMA((PARTS,)),
            pltpu.SemaphoreType.DMA((PARTS,)),
        ],
        compiler_params=pltpu.CompilerParams(vmem_limit_bytes=16 * MIB),
        name="finish_last",
    )(
        in_hbm(current), in_vmem(factor), parts, in_vmem(total), *received, in_vmem(couple), sep_idx, sep_count
    )


def hop(value, mask, size):
    return lax.ppermute(value, AXES, [(i, i ^ mask) for i in range(size)])


def choose_kernel(source, own, low, high, both, held):
    rows = own.shape[0]
    s = source[0]

    @pl.when(s == 0)
    def _():
        held[...] = own[...]

    for i, ref in enumerate((low, high, both)):

        @pl.when(s == i + 1)
        def _(ref=ref):
            held[...] = ref[rows:]


def choose(source, own, low, high, both):
    return pl.pallas_call(
        choose_kernel,
        out_shape=jax.ShapeDtypeStruct(own.shape, own.dtype),
        in_specs=[SMEM] + [VMEM] * 4,
        out_specs=VMEM,
        compiler_params=pltpu.CompilerParams(vmem_limit_bytes=2 * MIB),
        name="choose",
    )(source, own, low, high, both)


def exchange(sent, branch, source, size):
    own = sent[3]
    rows = own.shape[0]
    got = [hop(value, m, size) for value, m in zip(sent, (size - 1, size // 2, 1))]
    held = choose(source, own, got[2], got[1], got[0])
    branches = [lambda v: v] + [lambda v, m=m: hop(v, 2 * m, size) for m in range(1, size // 4)]
    third = lax.switch(branch[0], branches, held)
    return [got[0], got[1], third, got[2]]


def share(part):
    return lax.all_to_all(part, AXES, 0, 0, tiled=True)


def local(
    factor, prior, tile_src, tile_dst, tile_count, tile_vals, sep_idx, sep_count, couple, masks
):
    size = lax.axis_size(AXES)
    comps, nodes = factor.shape
    nodes_all = size * nodes
    idx, pairs = sep_idx[0], couple[0]
    live = tile_count.reshape(1, 1)
    packed, s0, s1, s3, own, source, branch, factor, start, pairs, vals = prepare(
        masks, factor, prior, pairs, tile_vals, idx, sep_count, size
    )
    received = exchange([s0, s1, s3, own], branch, source, size)
    total = tile_product(packed, tile_src, tile_dst, live, vals, comps, True)
    current, packed, part, *sent = finish_first(
        factor, start, total, received, pairs, idx, sep_count, size
    )
    parts = share(part)
    received = exchange(sent, branch, source, size)
    total = tile_product(packed, tile_src, tile_dst, live, tile_vals, 2 * comps, False)
    updated, part = finish_last(
        current, factor, parts, total, received, pairs, idx, sep_count, nodes_all
    )
    beta, energy = close(share(part), nodes_all)
    return updated, beta, energy


def solution(mesh):
    in_specs = (
        P(None, ("row", "col")),
        P(None, ("row", "col")),
        P(("row", "col"), None),
        P(("row", "col"), None),
        P(("row", "col")),
        P(("row", "col"), None, None),
        P(("row", "col"), None, None),
        P(("row", "col"), None),
        P(("row", "col"), None, None, None),
        P(),
    )
    out_specs = (P(None, ("row", "col")), P(), P())
    return jax.shard_map(local, mesh=mesh, in_specs=in_specs, out_specs=out_specs, check_vma=False)
```

```python
import jax
import jax.numpy as jnp
from jax import lax
from jax.experimental import pallas as pl
from jax.experimental.pallas import tpu as pltpu
from jax.sharding import PartitionSpec as P

TILE = 128
MOMENTUM_CAP = 0.9
BETA0 = 0.5 * MOMENTUM_CAP
AXES = ("row", "col")
MIB = 1024 * 1024
WIDE = 4
BATCH = 16
STRETCH_BITS = 5
STRETCH = 1 << STRETCH_BITS
GROUP = 96
SMEM = pl.BlockSpec(memory_space=pltpu.SMEM)
VMEM = pl.BlockSpec(memory_space=pltpu.VMEM)
HBM = pl.BlockSpec(memory_space=pltpu.HBM)
PARTS = 4


def in_hbm(x):
    return pltpu.with_memory_space_constraint(x, pltpu.HBM)


def in_vmem(x):
    return pltpu.with_memory_space_constraint(x, pltpu.VMEM)


def span(c):
    return pl.ds(pl.multiple_of(c * WIDE * TILE, WIDE * TILE), WIDE * TILE)


def identity(n):
    row = lax.broadcasted_iota(jnp.int32, (n, n), 0)
    return jnp.where(row == lax.broadcasted_iota(jnp.int32, (n, n), 1), 1.0, 0.0).astype(jnp.bfloat16)


def turn_into(rows_ref, c, eye, values):
    n = eye.shape[0]
    for i in range(values.shape[1] // n):
        turned = lax.dot_general(
            eye, values[:, i * n : (i + 1) * n], (((1,), (1,)), ((), ())),
            preferred_element_type=jnp.float32,
        )
        start = pl.multiple_of(c * WIDE * TILE + i * n, n)
        rows_ref[pl.ds(start, n), : values.shape[0]] = turned


def over_live(slots, live, body):
    def step(c, _):
        body(pl.multiple_of(c * STRETCH, STRETCH))
        return 0

    lax.fori_loop(0, jnp.minimum(lax.shift_right_logical(live + STRETCH - 1, STRETCH_BITS), slots // STRETCH), step, 0)


def copy_rows(node_rows, idx_smem, count_ref, slot_rows):
    rounds, slots = idx_smem.shape
    for k in range(rounds):

        def body(first, k=k):
            for q in range(0, STRETCH, BATCH):
                at = [idx_smem[k, first + q + j] for j in range(BATCH)]
                rows = [node_rows[pl.ds(at[j], 1), :] for j in range(BATCH)]
                for j in range(BATCH):
                    slot_rows[pl.ds(k * slots + first + q + j, 1), :] = rows[j]

        over_live(slots, count_ref[0, k], body)


def columns(slot_rows, k, count_ref, rows, comps, slots):
    got = slot_rows[k * slots : (k + 1) * slots, :].T[:rows]
    keep = lax.broadcasted_iota(jnp.int32, got.shape, 1) < count_ref[0, k]
    if rows > comps:
        keep = keep & (lax.broadcasted_iota(jnp.int32, got.shape, 0) < comps)
    return jnp.where(keep, got, 0.0).astype(jnp.bfloat16)


def emit(slot_rows, count_ref, outs, own, comps):
    rows, slots = own.shape
    shared = columns(slot_rows, 2, count_ref, rows, comps, slots)
    own[...] = shared
    for k, out in zip((0, 1, 3), outs):
        out[:rows] = columns(slot_rows, k, count_ref, rows, comps, slots)
        out[rows:] = shared


def part_copies(source, target, sems):
    width = source.shape[1] // PARTS
    return [
        pltpu.make_async_copy(
            source.at[:, pl.ds(i * width, width)], target.at[:, pl.ds(i * width, width)], sems.at[i]
        )
        for i in range(PARTS)
    ]


def prepare_kernel(size, masks, factor_hbm, prior_hbm, couple_hbm, vals_hbm, idx_smem, count_ref,
                   packed, s0, s1, s3, own, source, branch, factor, start, couple, vals,
                   node_rows, slot_rows, prior, sems, more_sems):
    f_copies = part_copies(factor_hbm, factor, sems.at[0])
    p_copies = part_copies(prior_hbm, prior, sems.at[1])
    for i in range(PARTS):
        f_copies[i].start()
        p_copies[i].start()
    each = vals.shape[0] // PARTS
    brought = [
        pltpu.make_async_copy(
            vals_hbm.at[pl.ds(i * each, each)], vals.at[pl.ds(i * each, each)], more_sems.at[i]
        )
        for i in range(PARTS)
    ]
    brought.append(pltpu.make_async_copy(couple_hbm, couple, more_sems.at[PARTS]))
    comps, nodes = factor.shape
    rows = packed.shape[1]
    mask = masks[2]
    top, bottom = (mask >= size // 2).astype(jnp.int32), mask & 1
    source[0] = 2 * top + bottom
    rest = jnp.where(top + bottom == 2, mask ^ (size - 1), mask)
    branch[0] = lax.shift_right_logical(rest & (size // 2 - 1), 1)
    pad = jnp.zeros((rows - comps, WIDE * TILE), jnp.float32)
    eye = identity(2 * TILE)

    def step(c, _):
        f = factor[:, span(c)]
        blend = f + BETA0 * (f - prior[:, span(c)])
        start[:, span(c)] = blend
        values = jnp.concatenate([blend, pad], axis=0).astype(packed.dtype)
        turn_into(node_rows, c, eye, values)
        for i in range(WIDE):
            packed[c * WIDE + i] = values[:, i * TILE : (i + 1) * TILE]
        return 0

    each = nodes // (WIDE * TILE * PARTS)
    for i in range(PARTS):
        f_copies[i].wait()
        p_copies[i].wait()
        if i == 0:
            for copy in brought:
                copy.start()
        lax.fori_loop(i * each, (i + 1) * each, step, 0, unroll=2)
    copy_rows(node_rows, idx_smem, count_ref, slot_rows)
    emit(slot_rows, count_ref, (s0, s1, s3), own, comps)
    for copy in brought:
        copy.wait()


def prepare(masks, factor, prior, couple, tile_vals, sep_idx, sep_count, size):
    comps, nodes = factor.shape
    rounds, slots = sep_idx.shape
    rows = 32

    def body(*refs):
        prepare_kernel(size, *refs)

    both = jax.ShapeDtypeStruct((2 * rows, slots), jnp.bfloat16)
    return pl.pallas_call(
        body,
        out_shape=[
            pltpu.VMEM((nodes // TILE, rows, TILE), jnp.bfloat16),
            both,
            both,
            both,
            jax.ShapeDtypeStruct((rows, slots), jnp.bfloat16),
            jax.ShapeDtypeStruct((1,), jnp.int32),
            jax.ShapeDtypeStruct((1,), jnp.int32),
            pltpu.VMEM((comps, nodes), jnp.float32),
            pltpu.VMEM((comps, nodes), jnp.float32),
            pltpu.VMEM(couple.shape, couple.dtype),
            pltpu.VMEM((tile_vals.shape[0] - GROUP, TILE, TILE), tile_vals.dtype),
        ],
        in_specs=[SMEM] + [HBM] * 4 + [SMEM, SMEM],
        out_specs=[VMEM] * 5 + [SMEM] * 2 + [VMEM] * 4,
        scratch_shapes=[
            pltpu.VMEM((nodes, TILE), jnp.float32),
            pltpu.VMEM((rounds * slots, TILE), jnp.float32),
            pltpu.VMEM((comps, nodes), jnp.float32),
            pltpu.SemaphoreType.DMA((2, PARTS)),
            pltpu.SemaphoreType.DMA((PARTS + 1,)),
        ],
        compiler_params=pltpu.CompilerParams(vmem_limit_bytes=20 * MIB),
        name="prepare",
    )(
        in_hbm(masks), in_hbm(factor), in_hbm(prior), in_hbm(couple), in_hbm(tile_vals),
        in_hbm(sep_idx), in_hbm(sep_count),
    )


def tile_steps(keep, group, arrive, src, dst, count, packed, vals, total, start=0):
    spare, rows, _ = packed.shape

    def one(g, _):
        arrive(g)
        base = g * group
        products = []
        for j in range(0, group, 2):
            left = jnp.concatenate(
                [packed[src[0, start + base + j]], packed[src[0, start + base + j + 1]]], axis=0
            )
            right = jnp.concatenate([vals[base + j], vals[base + j + 1]], axis=1)
            both = jnp.dot(left, right, preferred_element_type=jnp.float32)
            products += [both[:keep, :TILE], both[rows : rows + keep, TILE:]]
        for j in range(group):
            to = jnp.where(start + base + j < count[0, 0], dst[0, start + base + j], spare)
            total[to] += products[j]
        return 0

    lax.fori_loop(0, vals.shape[0] // group, one, 0)


def resident_kernel(keep, group, src, dst, count, packed, held, vals_hbm, total, rest, sems):
    first = held.shape[0]
    bring = pltpu.make_async_copy(vals_hbm.at[pl.ds(first, rest.shape[0])], rest, sems.at[0])
    bring.start()
    total[...] = jnp.zeros_like(total)
    tile_steps(keep, group, lambda g: None, src, dst, count, packed, held, total)
    bring.wait()
    tile_steps(keep, group, lambda g: None, src, dst, count, packed, rest, total, first)


def streamed_kernel(keep, group, src, dst, count, packed_hbm, vals_hbm, total, packed, vals, sems):
    groups = vals.shape[0] // group
    bring = pltpu.make_async_copy(packed_hbm, packed, sems.at[groups])
    bring.start()

    def tiles(g):
        at = pl.ds(g * group, group)
        return pltpu.make_async_copy(vals_hbm.at[at], vals.at[at], sems.at[g])

    for g in range(groups):
        tiles(g).start()
    total[...] = jnp.zeros_like(total)
    bring.wait()
    tile_steps(keep, group, lambda g: tiles(g).wait(), src, dst, count, packed, vals, total)


def tile_product(packed, tile_src, tile_dst, tile_count, tile_vals, keep, held=None):
    resident = held is not None
    blocks, rows, _ = packed.shape
    slots = tile_vals.shape[0]
    group = GROUP if resident else 64

    def body(*refs):
        (resident_kernel if resident else streamed_kernel)(keep, group, *refs)

    if resident:
        place, spec, kept = in_vmem, VMEM, [in_vmem(held)]
        scratch = [
            pltpu.VMEM((slots - held.shape[0], TILE, TILE), tile_vals.dtype),
            pltpu.SemaphoreType.DMA((1,)),
        ]
    else:
        place, spec, kept = in_hbm, HBM, []
        scratch = [
            pltpu.VMEM(packed.shape, packed.dtype),
            pltpu.VMEM(tile_vals.shape, tile_vals.dtype),
            pltpu.SemaphoreType.DMA((slots // group + 1,)),
        ]
    return pl.pallas_call(
        body,
        out_shape=pltpu.VMEM((blocks + 1, keep, TILE), jnp.float32),
        in_specs=[SMEM, SMEM, SMEM, spec] + [VMEM] * len(kept) + [HBM],
        out_specs=VMEM,
        scratch_shapes=scratch,
        compiler_params=pltpu.CompilerParams(vmem_limit_bytes=(12 if resident else 24) * MIB),
        cost_estimate=pl.CostEstimate(
            flops=2 * slots * rows * TILE * TILE,
            bytes_accessed=slots * TILE * TILE * 2 + blocks * rows * TILE * 8,
            transcendentals=0,
        ),
        name="tile_product",
    )(tile_src, tile_dst, tile_count, place(packed), *kept, in_hbm(tile_vals))


def scatter_rows(extra_rows, idx_smem, count_ref, spread):
    rounds, slots = idx_smem.shape
    spread[...] = jnp.zeros_like(spread)
    for k in range(rounds):

        def body(first, k=k):
            for q in range(0, STRETCH, BATCH):
                at = [idx_smem[k, first + q + j] for j in range(BATCH)]
                new = [
                    spread[pl.ds(at[j], 1), :] + extra_rows[pl.ds(k * slots + first + q + j, 1), :]
                    for j in range(BATCH)
                ]
                for j in range(BATCH):
                    spread[pl.ds(at[j], 1), :] = new[j]

        over_live(slots, count_ref[0, k], body)


def couple_rows(rows, received, couple, count_ref, extra_rows, combine):
    for k, ref in enumerate(received):
        slots = ref.shape[1]
        extra = combine(jnp.dot(ref[:rows], couple[k], preferred_element_type=jnp.float32))
        slot = lax.broadcasted_iota(jnp.int32, extra.shape, 1)
        extra = jnp.where(slot < count_ref[0, k], extra, 0.0)
        fill = jnp.zeros((TILE - extra.shape[0], slots), jnp.float32)
        extra_rows[k * slots : (k + 1) * slots, :] = jnp.concatenate([extra, fill], axis=0).T


def wide_total(total, c):
    return jnp.concatenate([total[c * WIDE + i] for i in range(WIDE)], axis=1)


def narrow(sums):
    return sum(sums[:, i * TILE : (i + 1) * TILE] for i in range(WIDE))


def fold(change, total):
    a = jnp.sum(change, axis=0, keepdims=True)
    b = jnp.sum(total, axis=0, keepdims=True)
    a = a + pltpu.roll(a, 64, 1)
    b = b + pltpu.roll(b, 64, 1)
    lane = lax.broadcasted_iota(jnp.int32, a.shape, 1)
    return jnp.where(lane < 64, a, b)


def first_kernel(factor, start, total, r0, r1, r2, r3, couple, idx_smem, count_ref,
                 updated_hbm, packed_hbm, part, s0, s1, s3, own, node_rows, slot_rows, updated, packed, sems):
    comps, nodes = factor.shape
    couple_rows(r2.shape[0], (r0, r1, r2, r3), couple, count_ref, slot_rows, lambda e: e[:comps])
    scatter_rows(slot_rows, idx_smem, count_ref, node_rows)
    eye = identity(2 * TILE)

    def step(c, sums):
        f = factor[:, span(c)]
        blend = start[:, span(c)]
        applied = wide_total(total, c) + node_rows[span(c), :].T[:comps]
        moved = blend + applied
        square = jnp.sum(moved * moved, axis=0, keepdims=True)
        u = moved * lax.rsqrt(jnp.maximum(square, 1.0))
        d = u - f
        updated[:, span(c)] = u
        both = jnp.concatenate([u + BETA0 * d, d], axis=0).astype(packed.dtype)
        turn_into(node_rows, c, eye, both)
        for i in range(WIDE):
            packed[c * WIDE + i] = both[:, i * TILE : (i + 1) * TILE]
        return sums + applied * d

    copies = part_copies(updated, updated_hbm, sems)
    sums = jnp.zeros((comps, WIDE * TILE), jnp.float32)
    each = nodes // (WIDE * TILE * PARTS)
    for i in range(PARTS):
        sums = lax.fori_loop(i * each, (i + 1) * each, step, sums, unroll=2)
        copies[i].start()
    copies.append(pltpu.make_async_copy(packed, packed_hbm, sems.at[PARTS]))
    copies[PARTS].start()
    sums = narrow(sums)
    part[...] = jnp.broadcast_to(fold(sums, sums), part.shape)
    copy_rows(node_rows, idx_smem, count_ref, slot_rows)
    emit(slot_rows, count_ref, (s0, s1, s3), own, 2 * comps)
    for copy in copies:
        copy.wait()


def finish_first(factor, start, total, received, couple, sep_idx, sep_count, parts):
    comps, nodes = factor.shape
    rounds, slots = sep_idx.shape
    f32 = jnp.float32
    packed = (nodes // TILE, 2 * comps, TILE)
    both = jax.ShapeDtypeStruct((4 * comps, slots), jnp.bfloat16)
    return pl.pallas_call(
        first_kernel,
        out_shape=[
            pltpu.HBM((comps, nodes), f32),
            pltpu.HBM(packed, jnp.bfloat16),
            jax.ShapeDtypeStruct((parts, TILE), f32),
            both,
            both,
            both,
            jax.ShapeDtypeStruct((2 * comps, slots), jnp.bfloat16),
        ],
        in_specs=[VMEM] * 8 + [SMEM, SMEM],
        out_specs=[HBM, HBM] + [VMEM] * 5,
        scratch_shapes=[
            pltpu.VMEM((nodes, TILE), f32),
            pltpu.VMEM((rounds * slots, TILE), f32),
            pltpu.VMEM((comps, nodes), f32),
            pltpu.VMEM(packed, jnp.bfloat16),
            pltpu.SemaphoreType.DMA((PARTS + 1,)),
        ],
        compiler_params=pltpu.CompilerParams(vmem_limit_bytes=16 * MIB),
        name="finish_first",
    )(
        in_vmem(factor), in_vmem(start), in_vmem(total), *received, in_vmem(couple), sep_idx, sep_count
    )


def beta_of(change, nodes_all):
    return MOMENTUM_CAP * 0.5 * (1.0 + jnp.tanh(change / nodes_all))


def last_kernel(nodes_all, current_hbm, factor, parts, total, r0, r1, r2, r3, couple, idx_smem, count_ref,
                updated_hbm, part, spread, extra_rows, current, updated, in_sems, sems):
    come = part_copies(current_hbm, current, in_sems)
    for copy in come:
        copy.start()
    comps, nodes = current.shape
    lane = lax.broadcasted_iota(jnp.int32, (1, TILE), 1)
    summed = jnp.sum(parts[...], axis=0, keepdims=True)
    change = jnp.sum(jnp.where(lane < 64, summed, 0.0), axis=1, keepdims=True)
    beta = beta_of(change, nodes_all)
    gap = beta - BETA0
    couple_rows(
        r2.shape[0], (r0, r1, r2, r3), couple, count_ref, extra_rows,
        lambda e: e[:comps] + gap * e[comps:],
    )
    scatter_rows(extra_rows, idx_smem, count_ref, spread)

    def step(c, sums):
        u = current[:, span(c)]
        blend = u + beta * (u - factor[:, span(c)])
        both = wide_total(total, c)
        applied = both[:comps] + gap * both[comps:] + spread[span(c), :].T[:comps]
        moved = blend + applied
        square = jnp.sum(moved * moved, axis=0, keepdims=True)
        new = moved * lax.rsqrt(jnp.maximum(square, 1.0))
        updated[:, span(c)] = new
        return sums[0] + applied * (new - u), sums[1] + applied * new

    zero = jnp.zeros((comps, WIDE * TILE), jnp.float32)
    sums = (zero, zero)
    leave = part_copies(updated, updated_hbm, sems)
    each = nodes // (WIDE * TILE * PARTS)
    for i in range(PARTS):
        come[i].wait()
        sums = lax.fori_loop(i * each, (i + 1) * each, step, sums, unroll=2)
        leave[i].start()
    part[...] = jnp.broadcast_to(fold(narrow(sums[0]), narrow(sums[1])), part.shape)
    for copy in leave:
        copy.wait()


def close_kernel(nodes_all, parts, momentum, energy):
    lane = lax.broadcasted_iota(jnp.int32, (1, TILE), 1)
    summed = jnp.sum(parts[...], axis=0, keepdims=True)
    change = jnp.sum(jnp.where(lane < 64, summed, 0.0), axis=1, keepdims=True)
    total = jnp.sum(jnp.where(lane < 64, 0.0, summed), axis=1, keepdims=True)
    momentum[0] = beta_of(change, nodes_all)[0, 0]
    energy[0] = (total / nodes_all)[0, 0]


def close(parts, nodes_all):
    def body(*refs):
        close_kernel(nodes_all, *refs)

    one = jax.ShapeDtypeStruct((1,), jnp.float32)
    momentum, energy = pl.pallas_call(
        body,
        out_shape=[one, one],
        in_specs=[VMEM],
        out_specs=[SMEM, SMEM],
        compiler_params=pltpu.CompilerParams(vmem_limit_bytes=2 * MIB),
        name="close",
    )(parts)
    return momentum.reshape(()), energy.reshape(())


def finish_last(current, factor, parts, total, received, couple, sep_idx, sep_count, nodes_all):
    comps, nodes = factor.shape
    rounds, slots = sep_idx.shape
    f32 = jnp.float32

    def body(*refs):
        last_kernel(nodes_all, *refs)

    return pl.pallas_call(
        body,
        out_shape=[
            pltpu.HBM((comps, nodes), f32),
            jax.ShapeDtypeStruct(parts.shape, f32),
        ],
        in_specs=[HBM] + [VMEM] * 8 + [SMEM, SMEM],
        out_specs=[HBM, VMEM],
        scratch_shapes=[
            pltpu.VMEM((nodes, TILE), f32),
            pltpu.VMEM((rounds * slots, TILE), f32),
            pltpu.VMEM((comps, nodes), f32),
            pltpu.VMEM((comps, nodes), f32),
            pltpu.SemaphoreType.DMA((PARTS,)),
            pltpu.SemaphoreType.DMA((PARTS,)),
        ],
        compiler_params=pltpu.CompilerParams(vmem_limit_bytes=16 * MIB),
        name="finish_last",
    )(
        in_hbm(current), in_vmem(factor), parts, in_vmem(total), *received, in_vmem(couple), sep_idx, sep_count
    )


def hop(value, mask, size):
    return lax.ppermute(value, AXES, [(i, i ^ mask) for i in range(size)])


def choose_kernel(source, own, low, high, both, held):
    rows = own.shape[0]
    s = source[0]

    @pl.when(s == 0)
    def _():
        held[...] = own[...]

    for i, ref in enumerate((low, high, both)):

        @pl.when(s == i + 1)
        def _(ref=ref):
            held[...] = ref[rows:]


def choose(source, own, low, high, both):
    return pl.pallas_call(
        choose_kernel,
        out_shape=jax.ShapeDtypeStruct(own.shape, own.dtype),
        in_specs=[SMEM] + [VMEM] * 4,
        out_specs=VMEM,
        compiler_params=pltpu.CompilerParams(vmem_limit_bytes=2 * MIB),
        name="choose",
    )(source, own, low, high, both)


def exchange(sent, branch, source, size):
    own = sent[3]
    rows = own.shape[0]
    got = [hop(value, m, size) for value, m in zip(sent, (size - 1, size // 2, 1))]
    held = choose(source, own, got[2], got[1], got[0])
    branches = [lambda v: v] + [lambda v, m=m: hop(v, 2 * m, size) for m in range(1, size // 4)]
    third = lax.switch(branch[0], branches, held)
    return [got[0], got[1], third, got[2]]


def share(part):
    return lax.all_to_all(part, AXES, 0, 0, tiled=True)


def local(
    factor, prior, tile_src, tile_dst, tile_count, tile_vals, sep_idx, sep_count, couple, masks
):
    size = lax.axis_size(AXES)
    comps, nodes = factor.shape
    nodes_all = size * nodes
    idx, pairs = sep_idx[0], couple[0]
    live = tile_count.reshape(1, 1)
    packed, s0, s1, s3, own, source, branch, factor, start, pairs, vals = prepare(
        masks, factor, prior, pairs, tile_vals, idx, sep_count, size
    )
    received = exchange([s0, s1, s3, own], branch, source, size)
    total = tile_product(packed, tile_src, tile_dst, live, tile_vals, comps, vals)
    current, packed, part, *sent = finish_first(
        factor, start, total, received, pairs, idx, sep_count, size
    )
    parts = share(part)
    received = exchange(sent, branch, source, size)
    total = tile_product(packed, tile_src, tile_dst, live, tile_vals, 2 * comps)
    updated, part = finish_last(
        current, factor, parts, total, received, pairs, idx, sep_count, nodes_all
    )
    beta, energy = close(share(part), nodes_all)
    return updated, beta, energy


def solution(mesh):
    in_specs = (
        P(None, ("row", "col")),
        P(None, ("row", "col")),
        P(("row", "col"), None),
        P(("row", "col"), None),
        P(("row", "col")),
        P(("row", "col"), None, None),
        P(("row", "col"), None, None),
        P(("row", "col"), None),
        P(("row", "col"), None, None, None),
        P(),
    )
    out_specs = (P(None, ("row", "col")), P(), P())
    return jax.shard_map(local, mesh=mesh, in_specs=in_specs, out_specs=out_specs, check_vma=False)
```

```python
import jax
import jax.numpy as jnp
from jax import lax
from jax.experimental import pallas as pl
from jax.experimental.pallas import tpu as pltpu
from jax.sharding import PartitionSpec as P

TILE = 128
MOMENTUM_CAP = 0.9
BETA0 = 0.5 * MOMENTUM_CAP
AXES = ("row", "col")
MIB = 1024 * 1024
WIDE = 4
BATCH = 16
STRETCH_BITS = 5
STRETCH = 1 << STRETCH_BITS
GROUP = 96
SMEM = pl.BlockSpec(memory_space=pltpu.SMEM)
VMEM = pl.BlockSpec(memory_space=pltpu.VMEM)
HBM = pl.BlockSpec(memory_space=pltpu.HBM)
PARTS = 8


def in_hbm(x):
    return pltpu.with_memory_space_constraint(x, pltpu.HBM)


def in_vmem(x):
    return pltpu.with_memory_space_constraint(x, pltpu.VMEM)


def span(c):
    return pl.ds(pl.multiple_of(c * WIDE * TILE, WIDE * TILE), WIDE * TILE)


def identity(n):
    row = lax.broadcasted_iota(jnp.int32, (n, n), 0)
    return jnp.where(row == lax.broadcasted_iota(jnp.int32, (n, n), 1), 1.0, 0.0).astype(jnp.bfloat16)


def turn_into(rows_ref, c, eye, values):
    n = eye.shape[0]
    for i in range(values.shape[1] // n):
        turned = lax.dot_general(
            eye, values[:, i * n : (i + 1) * n], (((1,), (1,)), ((), ())),
            preferred_element_type=jnp.float32,
        )
        start = pl.multiple_of(c * WIDE * TILE + i * n, n)
        rows_ref[pl.ds(start, n), : values.shape[0]] = turned


def over_live(slots, live, body):
    def step(c, _):
        body(pl.multiple_of(c * STRETCH, STRETCH))
        return 0

    lax.fori_loop(0, jnp.minimum(lax.shift_right_logical(live + STRETCH - 1, STRETCH_BITS), slots // STRETCH), step, 0)


def copy_rows(node_rows, idx_smem, count_ref, slot_rows):
    rounds, slots = idx_smem.shape
    for k in range(rounds):

        def body(first, k=k):
            for q in range(0, STRETCH, BATCH):
                at = [idx_smem[k, first + q + j] for j in range(BATCH)]
                rows = [node_rows[pl.ds(at[j], 1), :] for j in range(BATCH)]
                for j in range(BATCH):
                    slot_rows[pl.ds(k * slots + first + q + j, 1), :] = rows[j]

        over_live(slots, count_ref[0, k], body)


def columns(slot_rows, k, count_ref, rows, comps, slots):
    got = slot_rows[k * slots : (k + 1) * slots, :].T[:rows]
    keep = lax.broadcasted_iota(jnp.int32, got.shape, 1) < count_ref[0, k]
    if rows > comps:
        keep = keep & (lax.broadcasted_iota(jnp.int32, got.shape, 0) < comps)
    return jnp.where(keep, got, 0.0).astype(jnp.bfloat16)


def emit(slot_rows, count_ref, outs, own, comps):
    rows, slots = own.shape
    shared = columns(slot_rows, 2, count_ref, rows, comps, slots)
    own[...] = shared
    for k, out in zip((0, 1, 3), outs):
        out[:rows] = columns(slot_rows, k, count_ref, rows, comps, slots)
        out[rows:] = shared


def part_copies(source, target, sems):
    width = source.shape[1] // PARTS
    return [
        pltpu.make_async_copy(
            source.at[:, pl.ds(i * width, width)], target.at[:, pl.ds(i * width, width)], sems.at[i]
        )
        for i in range(PARTS)
    ]


def prepare_kernel(size, masks, factor_hbm, prior_hbm, couple_hbm, vals_hbm, idx_smem, count_ref,
                   packed, s0, s1, s3, own, source, branch, factor, start, couple, vals,
                   node_rows, slot_rows, prior, sems, more_sems):
    f_copies = part_copies(factor_hbm, factor, sems.at[0])
    p_copies = part_copies(prior_hbm, prior, sems.at[1])
    for i in range(PARTS):
        f_copies[i].start()
        p_copies[i].start()
    each = vals.shape[0] // PARTS
    brought = [
        pltpu.make_async_copy(
            vals_hbm.at[pl.ds(i * each, each)], vals.at[pl.ds(i * each, each)], more_sems.at[i]
        )
        for i in range(PARTS)
    ]
    brought.append(pltpu.make_async_copy(couple_hbm, couple, more_sems.at[PARTS]))
    comps, nodes = factor.shape
    rows = packed.shape[1]
    mask = masks[2]
    top, bottom = (mask >= size // 2).astype(jnp.int32), mask & 1
    source[0] = 2 * top + bottom
    rest = jnp.where(top + bottom == 2, mask ^ (size - 1), mask)
    branch[0] = lax.shift_right_logical(rest & (size // 2 - 1), 1)
    pad = jnp.zeros((rows - comps, WIDE * TILE), jnp.float32)
    eye = identity(2 * TILE)

    def step(c, _):
        f = factor[:, span(c)]
        blend = f + BETA0 * (f - prior[:, span(c)])
        start[:, span(c)] = blend
        values = jnp.concatenate([blend, pad], axis=0).astype(packed.dtype)
        turn_into(node_rows, c, eye, values)
        for i in range(WIDE):
            packed[c * WIDE + i] = values[:, i * TILE : (i + 1) * TILE]
        return 0

    each = nodes // (WIDE * TILE * PARTS)
    for i in range(PARTS):
        f_copies[i].wait()
        p_copies[i].wait()
        if i == 0:
            for copy in brought:
                copy.start()
        lax.fori_loop(i * each, (i + 1) * each, step, 0, unroll=2)
    copy_rows(node_rows, idx_smem, count_ref, slot_rows)
    emit(slot_rows, count_ref, (s0, s1, s3), own, comps)
    for copy in brought:
        copy.wait()


def prepare(masks, factor, prior, couple, tile_vals, sep_idx, sep_count, size):
    comps, nodes = factor.shape
    rounds, slots = sep_idx.shape
    rows = 32

    def body(*refs):
        prepare_kernel(size, *refs)

    both = jax.ShapeDtypeStruct((2 * rows, slots), jnp.bfloat16)
    return pl.pallas_call(
        body,
        out_shape=[
            pltpu.VMEM((nodes // TILE, rows, TILE), jnp.bfloat16),
            both,
            both,
            both,
            jax.ShapeDtypeStruct((rows, slots), jnp.bfloat16),
            jax.ShapeDtypeStruct((1,), jnp.int32),
            jax.ShapeDtypeStruct((1,), jnp.int32),
            pltpu.VMEM((comps, nodes), jnp.float32),
            pltpu.VMEM((comps, nodes), jnp.float32),
            pltpu.VMEM(couple.shape, couple.dtype),
            pltpu.VMEM((tile_vals.shape[0] - GROUP, TILE, TILE), tile_vals.dtype),
        ],
        in_specs=[SMEM] + [HBM] * 4 + [SMEM, SMEM],
        out_specs=[VMEM] * 5 + [SMEM] * 2 + [VMEM] * 4,
        scratch_shapes=[
            pltpu.VMEM((nodes, TILE), jnp.float32),
            pltpu.VMEM((rounds * slots, TILE), jnp.float32),
            pltpu.VMEM((comps, nodes), jnp.float32),
            pltpu.SemaphoreType.DMA((2, PARTS)),
            pltpu.SemaphoreType.DMA((PARTS + 1,)),
        ],
        compiler_params=pltpu.CompilerParams(vmem_limit_bytes=20 * MIB),
        name="prepare",
    )(
        in_hbm(masks), in_hbm(factor), in_hbm(prior), in_hbm(couple), in_hbm(tile_vals),
        in_hbm(sep_idx), in_hbm(sep_count),
    )


def tile_steps(keep, group, arrive, src, dst, count, packed, vals, total, start=0):
    spare, rows, _ = packed.shape

    def one(g, _):
        arrive(g)
        base = g * group
        products = []
        for j in range(0, group, 2):
            left = jnp.concatenate(
                [packed[src[0, start + base + j]], packed[src[0, start + base + j + 1]]], axis=0
            )
            right = jnp.concatenate([vals[base + j], vals[base + j + 1]], axis=1)
            both = jnp.dot(left, right, preferred_element_type=jnp.float32)
            products += [both[:keep, :TILE], both[rows : rows + keep, TILE:]]
        for j in range(group):
            to = jnp.where(start + base + j < count[0, 0], dst[0, start + base + j], spare)
            total[to] += products[j]
        return 0

    lax.fori_loop(0, vals.shape[0] // group, one, 0)


def resident_kernel(keep, group, src, dst, count, packed, held, vals_hbm, total, rest, sems):
    first = held.shape[0]
    bring = pltpu.make_async_copy(vals_hbm.at[pl.ds(first, rest.shape[0])], rest, sems.at[0])
    bring.start()
    total[...] = jnp.zeros_like(total)
    tile_steps(keep, group, lambda g: None, src, dst, count, packed, held, total)
    bring.wait()
    tile_steps(keep, group, lambda g: None, src, dst, count, packed, rest, total, first)


def streamed_kernel(keep, group, src, dst, count, packed_hbm, vals_hbm, total, packed, vals, sems):
    groups = vals.shape[0] // group
    bring = pltpu.make_async_copy(packed_hbm, packed, sems.at[groups])
    bring.start()

    def tiles(g):
        at = pl.ds(g * group, group)
        return pltpu.make_async_copy(vals_hbm.at[at], vals.at[at], sems.at[g])

    for g in range(groups):
        tiles(g).start()
    total[...] = jnp.zeros_like(total)
    bring.wait()
    tile_steps(keep, group, lambda g: tiles(g).wait(), src, dst, count, packed, vals, total)


def tile_product(packed, tile_src, tile_dst, tile_count, tile_vals, keep, held=None):
    resident = held is not None
    blocks, rows, _ = packed.shape
    slots = tile_vals.shape[0]
    group = GROUP if resident else 64

    def body(*refs):
        (resident_kernel if resident else streamed_kernel)(keep, group, *refs)

    if resident:
        place, spec, kept = in_vmem, VMEM, [in_vmem(held)]
        scratch = [
            pltpu.VMEM((slots - held.shape[0], TILE, TILE), tile_vals.dtype),
            pltpu.SemaphoreType.DMA((1,)),
        ]
    else:
        place, spec, kept = in_hbm, HBM, []
        scratch = [
            pltpu.VMEM(packed.shape, packed.dtype),
            pltpu.VMEM(tile_vals.shape, tile_vals.dtype),
            pltpu.SemaphoreType.DMA((slots // group + 1,)),
        ]
    return pl.pallas_call(
        body,
        out_shape=pltpu.VMEM((blocks + 1, keep, TILE), jnp.float32),
        in_specs=[SMEM, SMEM, SMEM, spec] + [VMEM] * len(kept) + [HBM],
        out_specs=VMEM,
        scratch_shapes=scratch,
        compiler_params=pltpu.CompilerParams(vmem_limit_bytes=(12 if resident else 24) * MIB),
        cost_estimate=pl.CostEstimate(
            flops=2 * slots * rows * TILE * TILE,
            bytes_accessed=slots * TILE * TILE * 2 + blocks * rows * TILE * 8,
            transcendentals=0,
        ),
        name="tile_product",
    )(tile_src, tile_dst, tile_count, place(packed), *kept, in_hbm(tile_vals))


def scatter_rows(extra_rows, idx_smem, count_ref, spread):
    rounds, slots = idx_smem.shape
    spread[...] = jnp.zeros_like(spread)
    for k in range(rounds):

        def body(first, k=k):
            for q in range(0, STRETCH, BATCH):
                at = [idx_smem[k, first + q + j] for j in range(BATCH)]
                new = [
                    spread[pl.ds(at[j], 1), :] + extra_rows[pl.ds(k * slots + first + q + j, 1), :]
                    for j in range(BATCH)
                ]
                for j in range(BATCH):
                    spread[pl.ds(at[j], 1), :] = new[j]

        over_live(slots, count_ref[0, k], body)


def couple_rows(rows, received, couple, count_ref, extra_rows, combine):
    for k, ref in enumerate(received):
        slots = ref.shape[1]
        extra = combine(jnp.dot(ref[:rows], couple[k], preferred_element_type=jnp.float32))
        slot = lax.broadcasted_iota(jnp.int32, extra.shape, 1)
        extra = jnp.where(slot < count_ref[0, k], extra, 0.0)
        fill = jnp.zeros((TILE - extra.shape[0], slots), jnp.float32)
        extra_rows[k * slots : (k + 1) * slots, :] = jnp.concatenate([extra, fill], axis=0).T


def wide_total(total, c):
    return jnp.concatenate([total[c * WIDE + i] for i in range(WIDE)], axis=1)


def narrow(sums):
    return sum(sums[:, i * TILE : (i + 1) * TILE] for i in range(WIDE))


def fold(change, total):
    a = jnp.sum(change, axis=0, keepdims=True)
    b = jnp.sum(total, axis=0, keepdims=True)
    a = a + pltpu.roll(a, 64, 1)
    b = b + pltpu.roll(b, 64, 1)
    lane = lax.broadcasted_iota(jnp.int32, a.shape, 1)
    return jnp.where(lane < 64, a, b)


def first_kernel(factor, start, total, r0, r1, r2, r3, couple, idx_smem, count_ref,
                 updated_hbm, packed_hbm, part, s0, s1, s3, own, node_rows, slot_rows, updated, packed, sems):
    comps, nodes = factor.shape
    couple_rows(r2.shape[0], (r0, r1, r2, r3), couple, count_ref, slot_rows, lambda e: e[:comps])
    scatter_rows(slot_rows, idx_smem, count_ref, node_rows)
    eye = identity(2 * TILE)

    def step(c, sums):
        f = factor[:, span(c)]
        blend = start[:, span(c)]
        applied = wide_total(total, c) + node_rows[span(c), :].T[:comps]
        moved = blend + applied
        square = jnp.sum(moved * moved, axis=0, keepdims=True)
        u = moved * lax.rsqrt(jnp.maximum(square, 1.0))
        d = u - f
        updated[:, span(c)] = u
        both = jnp.concatenate([u + BETA0 * d, d], axis=0).astype(packed.dtype)
        turn_into(node_rows, c, eye, both)
        for i in range(WIDE):
            packed[c * WIDE + i] = both[:, i * TILE : (i + 1) * TILE]
        return sums + applied * d

    copies = part_copies(updated, updated_hbm, sems)
    sums = jnp.zeros((comps, WIDE * TILE), jnp.float32)
    each = nodes // (WIDE * TILE * PARTS)
    for i in range(PARTS):
        sums = lax.fori_loop(i * each, (i + 1) * each, step, sums, unroll=2)
        copies[i].start()
    copies.append(pltpu.make_async_copy(packed, packed_hbm, sems.at[PARTS]))
    copies[PARTS].start()
    sums = narrow(sums)
    part[...] = jnp.broadcast_to(fold(sums, sums), part.shape)
    copy_rows(node_rows, idx_smem, count_ref, slot_rows)
    emit(slot_rows, count_ref, (s0, s1, s3), own, 2 * comps)
    for copy in copies:
        copy.wait()


def finish_first(factor, start, total, received, couple, sep_idx, sep_count, parts):
    comps, nodes = factor.shape
    rounds, slots = sep_idx.shape
    f32 = jnp.float32
    packed = (nodes // TILE, 2 * comps, TILE)
    both = jax.ShapeDtypeStruct((4 * comps, slots), jnp.bfloat16)
    return pl.pallas_call(
        first_kernel,
        out_shape=[
            pltpu.HBM((comps, nodes), f32),
            pltpu.HBM(packed, jnp.bfloat16),
            jax.ShapeDtypeStruct((parts, TILE), f32),
            both,
            both,
            both,
            jax.ShapeDtypeStruct((2 * comps, slots), jnp.bfloat16),
        ],
        in_specs=[VMEM] * 8 + [SMEM, SMEM],
        out_specs=[HBM, HBM] + [VMEM] * 5,
        scratch_shapes=[
            pltpu.VMEM((nodes, TILE), f32),
            pltpu.VMEM((rounds * slots, TILE), f32),
            pltpu.VMEM((comps, nodes), f32),
            pltpu.VMEM(packed, jnp.bfloat16),
            pltpu.SemaphoreType.DMA((PARTS + 1,)),
        ],
        compiler_params=pltpu.CompilerParams(vmem_limit_bytes=16 * MIB),
        name="finish_first",
    )(
        in_vmem(factor), in_vmem(start), in_vmem(total), *received, in_vmem(couple), sep_idx, sep_count
    )


def beta_of(change, nodes_all):
    return MOMENTUM_CAP * 0.5 * (1.0 + jnp.tanh(change / nodes_all))


def last_kernel(nodes_all, current_hbm, factor, parts, total, r0, r1, r2, r3, couple, idx_smem, count_ref,
                updated_hbm, part, spread, extra_rows, current, updated, in_sems, sems):
    come = part_copies(current_hbm, current, in_sems)
    for copy in come:
        copy.start()
    comps, nodes = current.shape
    lane = lax.broadcasted_iota(jnp.int32, (1, TILE), 1)
    summed = jnp.sum(parts[...], axis=0, keepdims=True)
    change = jnp.sum(jnp.where(lane < 64, summed, 0.0), axis=1, keepdims=True)
    beta = beta_of(change, nodes_all)
    gap = beta - BETA0
    couple_rows(
        r2.shape[0], (r0, r1, r2, r3), couple, count_ref, extra_rows,
        lambda e: e[:comps] + gap * e[comps:],
    )
    scatter_rows(extra_rows, idx_smem, count_ref, spread)

    def step(c, sums):
        u = current[:, span(c)]
        blend = u + beta * (u - factor[:, span(c)])
        both = wide_total(total, c)
        applied = both[:comps] + gap * both[comps:] + spread[span(c), :].T[:comps]
        moved = blend + applied
        square = jnp.sum(moved * moved, axis=0, keepdims=True)
        new = moved * lax.rsqrt(jnp.maximum(square, 1.0))
        updated[:, span(c)] = new
        return sums[0] + applied * (new - u), sums[1] + applied * new

    zero = jnp.zeros((comps, WIDE * TILE), jnp.float32)
    sums = (zero, zero)
    leave = part_copies(updated, updated_hbm, sems)
    each = nodes // (WIDE * TILE * PARTS)
    for i in range(PARTS):
        come[i].wait()
        sums = lax.fori_loop(i * each, (i + 1) * each, step, sums, unroll=2)
        leave[i].start()
    part[...] = jnp.broadcast_to(fold(narrow(sums[0]), narrow(sums[1])), part.shape)
    for copy in leave:
        copy.wait()


def close_kernel(nodes_all, parts, momentum, energy):
    lane = lax.broadcasted_iota(jnp.int32, (1, TILE), 1)
    summed = jnp.sum(parts[...], axis=0, keepdims=True)
    change = jnp.sum(jnp.where(lane < 64, summed, 0.0), axis=1, keepdims=True)
    total = jnp.sum(jnp.where(lane < 64, 0.0, summed), axis=1, keepdims=True)
    momentum[0] = beta_of(change, nodes_all)[0, 0]
    energy[0] = (total / nodes_all)[0, 0]


def close(parts, nodes_all):
    def body(*refs):
        close_kernel(nodes_all, *refs)

    one = jax.ShapeDtypeStruct((1,), jnp.float32)
    momentum, energy = pl.pallas_call(
        body,
        out_shape=[one, one],
        in_specs=[VMEM],
        out_specs=[SMEM, SMEM],
        compiler_params=pltpu.CompilerParams(vmem_limit_bytes=2 * MIB),
        name="close",
    )(parts)
    return momentum.reshape(()), energy.reshape(())


def finish_last(current, factor, parts, total, received, couple, sep_idx, sep_count, nodes_all):
    comps, nodes = factor.shape
    rounds, slots = sep_idx.shape
    f32 = jnp.float32

    def body(*refs):
        last_kernel(nodes_all, *refs)

    return pl.pallas_call(
        body,
        out_shape=[
            pltpu.HBM((comps, nodes), f32),
            jax.ShapeDtypeStruct(parts.shape, f32),
        ],
        in_specs=[HBM] + [VMEM] * 8 + [SMEM, SMEM],
        out_specs=[HBM, VMEM],
        scratch_shapes=[
            pltpu.VMEM((nodes, TILE), f32),
            pltpu.VMEM((rounds * slots, TILE), f32),
            pltpu.VMEM((comps, nodes), f32),
            pltpu.VMEM((comps, nodes), f32),
            pltpu.SemaphoreType.DMA((PARTS,)),
            pltpu.SemaphoreType.DMA((PARTS,)),
        ],
        compiler_params=pltpu.CompilerParams(vmem_limit_bytes=16 * MIB),
        name="finish_last",
    )(
        in_hbm(current), in_vmem(factor), parts, in_vmem(total), *received, in_vmem(couple), sep_idx, sep_count
    )


def hop(value, mask, size):
    return lax.ppermute(value, AXES, [(i, i ^ mask) for i in range(size)])


def choose_kernel(source, own, low, high, both, held):
    rows = own.shape[0]
    s = source[0]

    @pl.when(s == 0)
    def _():
        held[...] = own[...]

    for i, ref in enumerate((low, high, both)):

        @pl.when(s == i + 1)
        def _(ref=ref):
            held[...] = ref[rows:]


def choose(source, own, low, high, both):
    return pl.pallas_call(
        choose_kernel,
        out_shape=jax.ShapeDtypeStruct(own.shape, own.dtype),
        in_specs=[SMEM] + [VMEM] * 4,
        out_specs=VMEM,
        compiler_params=pltpu.CompilerParams(vmem_limit_bytes=2 * MIB),
        name="choose",
    )(source, own, low, high, both)


def exchange(sent, branch, source, size):
    own = sent[3]
    rows = own.shape[0]
    got = [hop(value, m, size) for value, m in zip(sent, (size - 1, size // 2, 1))]
    held = choose(source, own, got[2], got[1], got[0])
    branches = [lambda v: v] + [lambda v, m=m: hop(v, 2 * m, size) for m in range(1, size // 4)]
    third = lax.switch(branch[0], branches, held)
    return [got[0], got[1], third, got[2]]


def share(part):
    return lax.all_to_all(part, AXES, 0, 0, tiled=True)


def local(
    factor, prior, tile_src, tile_dst, tile_count, tile_vals, sep_idx, sep_count, couple, masks
):
    size = lax.axis_size(AXES)
    comps, nodes = factor.shape
    nodes_all = size * nodes
    idx, pairs = sep_idx[0], couple[0]
    live = tile_count.reshape(1, 1)
    packed, s0, s1, s3, own, source, branch, factor, start, pairs, vals = prepare(
        masks, factor, prior, pairs, tile_vals, idx, sep_count, size
    )
    received = exchange([s0, s1, s3, own], branch, source, size)
    total = tile_product(packed, tile_src, tile_dst, live, tile_vals, comps, vals)
    current, packed, part, *sent = finish_first(
        factor, start, total, received, pairs, idx, sep_count, size
    )
    parts = share(part)
    received = exchange(sent, branch, source, size)
    total = tile_product(packed, tile_src, tile_dst, live, tile_vals, 2 * comps)
    updated, part = finish_last(
        current, factor, parts, total, received, pairs, idx, sep_count, nodes_all
    )
    beta, energy = close(share(part), nodes_all)
    return updated, beta, energy


def solution(mesh):
    in_specs = (
        P(None, ("row", "col")),
        P(None, ("row", "col")),
        P(("row", "col"), None),
        P(("row", "col"), None),
        P(("row", "col")),
        P(("row", "col"), None, None),
        P(("row", "col"), None, None),
        P(("row", "col"), None),
        P(("row", "col"), None, None, None),
        P(),
    )
    out_specs = (P(None, ("row", "col")), P(), P())
    return jax.shard_map(local, mesh=mesh, in_specs=in_specs, out_specs=out_specs, check_vma=False)
```
